512 devices in a mesh: gx: 128 (over y, z, core), gy: 4 (over x).
Axes of the slice: x: 4, y: 8, z: 8, core: 2. Of those that a mesh axis runs over, the one named last changes fastest.
Arguments:
- multipoles: float32 [32768, 512], P(('gx', 'gy')), may hold values from -0.3125 to 0.3125
- occupancy: int32 [262144], P(('gx', 'gy')), may hold values 0 or 1
Outputs:
- far_field: float32 [32768, 512], P(('gx', 'gy'))
The draws below stay inside these ranges and needn't reach their ends.
All inputs are finite; a program needn't handle non-finite values. No bound on the sum of `occupancy` on one device may be relied on, other than what follows from the above.
Results may differ from the reference program's by a relative error of at most 0.0003.
Values sent between devices are 32-bit elements; how exact they have to be, the bound alone decides.
No kernel may reach another device: no remote copies, remote signals or barrier semaphores. Data moves between devices by JAX's collectives and lax.ppermute only.
A program may use at most 64 MiB of HBM per device.

```python
import math
import jax
import jax.numpy as jnp
from jax import lax

COEF = 64
DEPTH = 3
BOXES = 262144
GROUPS = 32768
N_GX = 128
N_GY = 4


def place_ends(values, own_key, least, top_value):
    shape = values.shape
    index_at = [jax.random.randint(jax.random.fold_in(own_key, axis), (), 0, shape[axis]) for axis in range(len(shape))]
    values = values.at[tuple(index_at)].set(least)
    longest = shape.index(max(shape))
    index_at[longest] = (index_at[longest] + 1) % shape[longest]
    return values.at[tuple(index_at)].set(top_value)


def level_of(key, dims, split, smallest, largest):
    def one(position, shards_of):
        heights = jax.random.uniform(jax.random.fold_in(jax.random.fold_in(key, 6), position), (shards_of,), jnp.float32, smallest / len(split), largest / len(split))
        return jnp.repeat(jnp.exp(heights), dims[position] // shards_of).reshape((-1,) + (1,) * (len(dims) - position - 1))

    level = one(*split[0])
    for cut in split[1:]:
        level = level * one(*cut)
    return level


def bell_draw(key, shape, deviation, bound, pieces=(), kind=jnp.bfloat16):
    values = jax.random.normal(key, shape, jnp.float32) * deviation
    if len(pieces) > 0:
        values = level_of(key, shape, pieces, -0.22, 0.18) * values
    return jnp.clip(values, min=-bound, max=bound).astype(kind)


def setup_inputs(seed: int = 0) -> dict:
    keys = jax.random.split(jax.random.key(seed), 3)
    return {
        "multipoles": bell_draw(keys[0], (GROUPS, 8 * COEF), 0.02, 0.3125, ((0, 512),), jnp.float32),
        "occupancy": place_ends((jax.random.randint(keys[1], (BOXES,), 0, 4) < 3).astype(jnp.int32), jax.random.fold_in(keys[1], 1), 0, 1),
    }


def exact_dot(left, right):
    return jnp.dot(left, right, precision=lax.Precision.HIGHEST)

def chebyshev_nodes():
    return jnp.cos((2.0 * jnp.arange(4, dtype=jnp.float32) + 1.0) * (math.pi / 8.0))

def degree_split(entries):
    return [entries // 16, entries // 4 % 4, entries % 4]

def octant_split(entries):
    return [entries // 2 ** axis_num % 2 for axis_num in range(3)]

def node_layout():
    entries = jnp.arange(512, dtype=jnp.int32)
    return (octant_split(entries // 64), degree_split(entries % 64))

def far_table(shift_x, shift_y, shift_z):
    node_values = chebyshev_nodes()
    octants, degrees = node_layout()
    shifts = [shift_x, shift_y, shift_z]
    distance = jnp.zeros((512, 512), jnp.float32)
    reach_max = jnp.zeros((512, 512), jnp.int32)
    for axis_num in range(3):
        offset = 2 * shifts[axis_num] + octants[axis_num][:, None] - octants[axis_num][None, :]
        reach_max = jnp.maximum(reach_max, jnp.abs(offset))
        placed = node_values[degrees[axis_num]]
        spread = offset.astype(jnp.float32) + 0.5 * (placed[:, None] - placed[None, :])
        distance = distance + spread * spread
    keep_mask = (reach_max >= 2).astype(jnp.float32)
    return keep_mask * lax.rsqrt(distance + (1.0 - keep_mask))

def chebyshev_terms(values):
    return [values, 2.0 * values * values - 1.0, 4.0 * values * values * values - 3.0 * values]

def interp_weight(first, second):
    result = 0.25 + 0.0 * first * second
    for left_term, right_term in zip(chebyshev_terms(first), chebyshev_terms(second)):
        result = result + 0.5 * left_term * right_term
    return result

def upward_matrix():
    node_values = chebyshev_nodes()
    octants, degrees = node_layout()
    parents = degree_split(jnp.arange(64, dtype=jnp.int32))
    result = jnp.ones((512, 64), jnp.float32)
    for axis_num in range(3):
        child_place = octants[axis_num].astype(jnp.float32) - 0.5 + 0.5 * node_values[degrees[axis_num]]
        parent_place = node_values[parents[axis_num]]
        result = result * interp_weight(parent_place[None, :], child_place[:, None])
    return result

def grid_order(bit_count):
    ordering = []
    extents = []
    for axis_num in range(3):
        owned = [level_bit for level_bit in range(bit_count) if level_bit % 3 == axis_num]
        ordering = ordering + [bit_count - 1 - level_bit for level_bit in reversed(owned)]
        extents.append(2 ** len(owned))
    return (ordering, extents)

def morton_to_grid(flat_rows, bit_count):
    row_width = flat_rows.shape[-1]
    ordering, extents = grid_order(bit_count)
    split_bits = flat_rows.reshape([2] * bit_count + [row_width])
    return jnp.transpose(split_bits, ordering + [bit_count]).reshape(extents + [row_width])

def grid_to_morton(grid_cells, bit_count):
    row_width = grid_cells.shape[-1]
    ordering, extents = grid_order(bit_count)
    split_bits = grid_cells.reshape([2] * bit_count + [row_width])
    inverse = [ordering.index(bit_place) for bit_place in range(bit_count)]
    return jnp.transpose(split_bits, inverse + [bit_count]).reshape(-1, row_width)

def morton_coords(numbers, bit_count):
    coords_list = []
    for axis_num in range(3):
        coordinate = 0 * numbers
        for level_bit in range(axis_num, bit_count, 3):
            coordinate = coordinate + numbers // 2 ** level_bit % 2 * 2 ** (level_bit // 3)
        coords_list.append(coordinate)
    return coords_list

def level_two(weights_two, target):
    count_boxes = weights_two.shape[0]
    bit_count = count_boxes.bit_length() - 1
    node_values = chebyshev_nodes()
    degrees = degree_split(jnp.arange(64, dtype=jnp.int32))
    sources = morton_coords(jnp.arange(count_boxes, dtype=jnp.int32), bit_count)
    targets = morton_coords(target, bit_count)
    keep_mask = jnp.ones((count_boxes,), jnp.float32)
    reach_max = jnp.zeros((count_boxes,), jnp.int32)
    distance = jnp.zeros((count_boxes, 64, 64), jnp.float32)
    for axis_num in range(3):
        offset = sources[axis_num] - targets[axis_num]
        parent_gap = sources[axis_num] // 2 - targets[axis_num] // 2
        keep_mask = keep_mask * (jnp.abs(parent_gap) <= 1).astype(jnp.float32)
        reach_max = jnp.maximum(reach_max, jnp.abs(offset))
        placed = node_values[degrees[axis_num]]
        spread = offset.astype(jnp.float32)[:, None, None] + 0.5 * (placed[None, :, None] - placed[None, None, :])
        distance = distance + spread * spread
    keep_mask = keep_mask * (reach_max >= 2).astype(jnp.float32)
    kernel = keep_mask[:, None, None] * lax.rsqrt(distance + (1.0 - keep_mask)[:, None, None])
    return jnp.einsum('uj,uji->i', weights_two, kernel, precision=lax.Precision.HIGHEST)

def reference(multipoles, occupancy):
    finest = 3 + DEPTH
    upward = upward_matrix()
    device_bits = (N_GX * N_GY).bit_length() - 1
    occupied = occupancy.astype(jnp.float32).reshape(-1, 8, 1)
    grouped = {finest: (multipoles.reshape(-1, 8, 64) * occupied).reshape(-1, 512)}
    for level_num in range(finest, 3, -1):
        grouped[level_num - 1] = exact_dot(grouped[level_num], upward).reshape(-1, 512)
    weights_two = exact_dot(grouped[3], upward)
    far_terms = {}
    for level_num in range(finest, 2, -1):
        bit_count = device_bits + 3 * (level_num - 4)
        grid_cells = morton_to_grid(grouped[level_num], bit_count)
        extents = grid_cells.shape[:3]
        padded = jnp.pad(grid_cells, ((1, 1), (1, 1), (1, 1), (0, 0)))
        accumulated = jnp.zeros((extents[0] * extents[1] * extents[2], 512), jnp.float32)
        for shift_step in range(27):
            shift_x = shift_step // 9 - 1
            shift_y = shift_step // 3 % 3 - 1
            shift_z = shift_step % 3 - 1
            source_rows = padded[1 + shift_x:1 + shift_x + extents[0], 1 + shift_y:1 + shift_y + extents[1], 1 + shift_z:1 + shift_z + extents[2]].reshape(-1, 512)
            accumulated = accumulated + exact_dot(source_rows, far_table(shift_x, shift_y, shift_z))
        far_terms[level_num] = grid_to_morton(accumulated.reshape(tuple(extents) + (512,)), bit_count) * 2.0 ** (level_num - finest)
    local_rows = lax.map(lambda target: level_two(weights_two, target), jnp.arange(weights_two.shape[0], dtype=jnp.int32)) * 2.0 ** (2 - finest)
    for level_num in range(3, finest + 1):
        local_rows = (far_terms[level_num] + exact_dot(local_rows, upward.T)).reshape(-1, 64)
    return (local_rows.reshape(-1, 8, 64) * occupied).reshape(-1, 512)
```

```python
import functools

import jax
import jax.numpy as jnp
import ml_dtypes
import numpy as np
from jax import lax
from jax.experimental import pallas as pl
from jax.experimental.pallas import tpu as pltpu
from jax.sharding import Mesh
from jax.sharding import PartitionSpec as P

F32 = jnp.float32
BF16 = jnp.bfloat16
NODES = np.cos((2.0 * np.arange(4) + 1.0) * (np.pi / 8.0))
ENTRY = np.arange(512)
OCT = [ENTRY // 64 % 2, ENTRY // 128 % 2, ENTRY // 256 % 2]
DEG = [ENTRY // 16 % 4, ENTRY // 4 % 4, ENTRY % 4]
KINDS = [(dx, ky, kz) for dx in (-1, 0, 1) for ky in range(3) for kz in range(3)]
ROWS = 80
SOURCES = 384


def halves(values):
    high = values.astype(np.float32).astype(ml_dtypes.bfloat16)
    low = (values - high.astype(np.float64)).astype(ml_dtypes.bfloat16)
    return high, low


def table(shift):
    distance = np.zeros((512, 512))
    reach = np.zeros((512, 512), int)
    for d in range(3):
        offset = 2 * shift[d] + OCT[d][:, None] - OCT[d][None, :]
        reach = np.maximum(reach, abs(offset))
        placed = NODES[DEG[d]]
        distance += (offset + 0.5 * (placed[:, None] - placed[None, :])) ** 2
    keep = reach >= 2
    return np.where(keep, 1.0 / np.sqrt(np.where(keep, distance, 1.0)), 0.0)


def upward_matrix():
    def terms(v):
        return [v, 2 * v * v - 1, 4 * v**3 - 3 * v]

    parent = np.arange(64)
    degrees = [parent // 16, parent // 4 % 4, parent % 4]
    result = np.ones((512, 64))
    for d in range(3):
        child = (OCT[d] - 0.5 + 0.5 * NODES[DEG[d]])[:, None]
        place = NODES[degrees[d]][None, :]
        result *= 0.25 + 0.5 * sum(a * b for a, b in zip(terms(place), terms(child)))
    return result


def parity_basis():
    basis = np.zeros((512, 512))
    for q in range(512):
        cy, cz = q // 128 % 2, q // 256
        ox, a, vy, vz = q // 64 % 2, q // 16 % 4, q // 4 % 4, q % 4
        for oy in range(2):
            for oz in range(2):
                b = 3 - vy if oy else vy
                e = 3 - vz if oz else vz
                sign = (-1) ** (cy * oy + cz * oz)
                basis[64 * (ox + 2 * oy + 4 * oz) + 16 * a + 4 * b + e, q] = 0.5 * sign
    return basis


def morton(x, y, z, bits):
    return sum(
        (x >> i & 1) << 3 * i | (y >> i & 1) << 3 * i + 1 | (z >> i & 1) << 3 * i + 2
        for i in range(bits)
    )


def place(number, bits):
    return [sum((number >> 3 * i + d & 1) << i for i in range(bits)) for d in range(3)]


Z_BASE, Y_BASE, X_BASE = 80, 128, 208
Z_ROWS, Y_ROWS, X_ROWS = 24, 40, 64


def level_extent(level):
    return 2 ** (level - 4)


def own_row(level, x, y, z):
    return {6: 0, 5: 64, 4: 72}[level] + morton(x, y, z, level - 4)


def z_row(level, x, y):
    n = level_extent(level)
    return {6: 0, 5: 16, 4: 20}[level] + y * n + x


def y_row(level, x, z):
    n = level_extent(level)
    return {6: 0, 5: 24, 4: 32}[level] + (z + 1) * n + x


def x_row(level, y, z):
    n = level_extent(level) + 2
    return {6: 0, 5: 36, 4: 52}[level] + (z + 1) * n + y + 1


def source_row(level, x, y, z):
    n = level_extent(level)
    if not 0 <= x < n:
        return X_BASE + (X_ROWS if x >= n else 0) + x_row(level, y, z)
    if not 0 <= y < n:
        return Y_BASE + (Y_ROWS if y >= n else 0) + y_row(level, x, z)
    if not 0 <= z < n:
        return Z_BASE + (Z_ROWS if z >= n else 0) + z_row(level, x, y)
    return own_row(level, x, y, z)


def kind_terms(kind):
    return [(0, 1)] if kind == 0 else [(1, 1), (-1, 1 if kind == 1 else -1)]


def selections():
    near = np.zeros((27, ROWS, SOURCES))
    for k, (dx, ky, kz) in enumerate(KINDS):
        for dy, sy in kind_terms(ky):
            for dz, sz in kind_terms(kz):
                for level in (6, 5, 4):
                    n = level_extent(level)
                    for m in range(n**3):
                        x, y, z = place(m, level - 4)
                        row = own_row(level, x, y, z)
                        near[k, row, source_row(level, x + dx, y + dy, z + dz)] += (
                            sy * sz * 2.0 ** (level - 6)
                        )
    coarse = np.zeros((64, 27, 8, 128))
    for parent in range(64):
        for level, row, base in ((3, 1, 0), (2, 2, 64)):
            bits = level - 1
            n = 2**bits
            x, y, z = place(parent >> 3 * (2 - bits), bits)
            for k, (dx, ky, kz) in enumerate(KINDS):
                for dy, sy in kind_terms(ky):
                    for dz, sz in kind_terms(kz):
                        u = (x + dx, y + dy, z + dz)
                        if all(0 <= c < n for c in u):
                            coarse[parent, k, row, base + morton(*u, bits)] += (
                                sy * sz * 2.0 ** (level - 6)
                            )
    return (
        near.reshape(27 * ROWS, SOURCES).astype(ml_dtypes.bfloat16),
        coarse.reshape(64, 216, 128).astype(ml_dtypes.bfloat16),
    )


@functools.lru_cache(maxsize=1)
def constants():
    basis = parity_basis()
    tables = {
        (dx, dy, dz): basis.T @ table((dx, dy, dz)) @ basis
        for dx in (-1, 0, 1)
        for dy in (0, 1)
        for dz in (0, 1)
    }
    far = np.zeros((4, 27 * 128, 256), ml_dtypes.bfloat16)
    for t in range(4):
        for k, (dx, ky, kz) in enumerate(KINDS):
            c = source_class(t, ky, kz)
            block = tables[dx, min(ky, 1), min(kz, 1)][
                128 * c : 128 * c + 128, 128 * t : 128 * t + 128
            ]
            high, low = halves(block)
            far[t, 128 * k : 128 * k + 128, :128] = high
            far[t, 128 * k : 128 * k + 128, 128:] = low
    up = upward_matrix()
    tiled = np.tile(up, (1, 8))
    down = np.tile(up.T, (8, 1))
    spread = (ENTRY[:, None] % 8 == ENTRY[None, :] // 64).astype(ml_dtypes.bfloat16)
    near, coarse = selections()
    return {
        "basis": basis.astype(ml_dtypes.bfloat16),
        "back": basis.T.astype(ml_dtypes.bfloat16),
        "up": np.concatenate(halves(tiled), axis=1),
        "down": np.concatenate(halves(down), axis=1),
        "spread": spread,
        "far": far,
        "near": near,
        "coarse": coarse,
    }


def source_class(t, ky, kz):
    return t ^ ((ky == 2) | (kz == 2) << 1)


def split(values):
    high = values.astype(BF16)
    return high, (values - high.astype(F32)).astype(BF16)


def mm(a, b):
    return jnp.dot(a, b, preferred_element_type=F32)


def stacked(values):
    rows = values.shape[0]
    if rows % 16:
        values = jnp.concatenate([values, jnp.zeros((16 - rows % 16, 512), F32)], axis=0)
    return jnp.concatenate(split(values), axis=0)


def times_exact(values, matrix):
    product = mm(stacked(values), matrix)
    half = product.shape[0] // 2
    return (product[:half] + product[half:])[: values.shape[0]]


def times_pair(values, matrix):
    product = mm(stacked(values), matrix)
    half = product.shape[0] // 2
    width = product.shape[1] // 2
    total = product[:half, :width] + product[half:, :width] + product[:half, width:]
    return total[: values.shape[0]]


def octant_mask(rows, offset):
    lane = lax.broadcasted_iota(jnp.int32, (rows, 512), 1) // 64
    row = lax.broadcasted_iota(jnp.int32, (rows, 512), 0)
    return (lane == (row + offset) % 8).astype(F32)


def occupancy_mask(occ_ref, spread_ref):
    lane = lax.broadcasted_iota(jnp.int32, (64, 512), 1) // 8
    row = lax.broadcasted_iota(jnp.int32, (64, 512), 0)
    occ = jnp.broadcast_to(occ_ref[...].astype(F32), (64, 512))
    return mm(jnp.where(lane == row, occ, 0.0).astype(BF16), spread_ref[...])


def up_group(values, up):
    rows = values.shape[0]
    return (times_pair(values, up) * octant_mask(rows, 0)).reshape(rows // 8, 8, 512).sum(axis=1)


def upward_kernel(ids_ref, mult_ref, occ_ref, spread_ref, basis_ref, up_ref, own_ref, pa_ref, pb_ref, three_ref):
    grouped_six = mult_ref[...] * occupancy_mask(occ_ref, spread_ref)
    grouped_five = up_group(grouped_six, up_ref[...])
    grouped_four = up_group(grouped_five, up_ref[...])
    three = times_pair(jnp.broadcast_to(grouped_four, (8, 512)), up_ref[...])
    three_ref[...] = three[:, :128]
    own_ref[0:64] = times_exact(grouped_six, basis_ref[...])
    rest = jnp.concatenate([grouped_five, jnp.broadcast_to(grouped_four, (8, 512))], axis=0)
    own_ref[64:80] = times_exact(rest, basis_ref[...])
    odd = ids_ref[2] == 1
    pa_ref[...] = jnp.zeros_like(pa_ref)
    pb_ref[...] = jnp.zeros_like(pb_ref)
    for level in (6, 5, 4):
        n = level_extent(level)
        for y in range(n):
            for x in range(n):
                low = own_ref[pl.ds(own_row(level, x, y, 0), 1)]
                high = own_ref[pl.ds(own_row(level, x, y, n - 1), 1)]
                i = z_row(level, x, y)
                pa_ref[pl.ds(i, 1)] = jnp.where(odd, low, high)
                pb_ref[pl.ds(i, 1)] = jnp.where(odd, high, low)


def sort_sides(odd, ra_ref, rb_ref, low_ref, high_ref):
    a, b = ra_ref[...], rb_ref[...]
    low_ref[...] = jnp.where(odd, a, b)
    high_ref[...] = jnp.where(odd, b, a)


def y_kernel(ids_ref, own_ref, za_ref, zb_ref, pa_ref, pb_ref, zl, zh):
    sort_sides(ids_ref[2] == 1, za_ref, zb_ref, zl, zh)
    odd = ids_ref[1] == 1
    pa_ref[...] = jnp.zeros_like(pa_ref)
    pb_ref[...] = jnp.zeros_like(pb_ref)

    def get(level, x, y, z):
        n = level_extent(level)
        if z < 0:
            return zl[pl.ds(z_row(level, x, y), 1)]
        if z >= n:
            return zh[pl.ds(z_row(level, x, y), 1)]
        return own_ref[pl.ds(own_row(level, x, y, z), 1)]

    for level in (6, 5, 4):
        n = level_extent(level)
        for z in range(-1, n + 1):
            for x in range(n):
                low, high = get(level, x, 0, z), get(level, x, n - 1, z)
                i = y_row(level, x, z)
                pa_ref[pl.ds(i, 1)] = jnp.where(odd, low, high)
                pb_ref[pl.ds(i, 1)] = jnp.where(odd, high, low)


def x_kernel(ids_ref, own_ref, za_ref, zb_ref, ya_ref, yb_ref, pa_ref, pb_ref, zl, zh, yl, yh):
    sort_sides(ids_ref[2] == 1, za_ref, zb_ref, zl, zh)
    sort_sides(ids_ref[1] == 1, ya_ref, yb_ref, yl, yh)
    odd = ids_ref[0] == 1
    pa_ref[...] = jnp.zeros_like(pa_ref)
    pb_ref[...] = jnp.zeros_like(pb_ref)

    def get(level, x, y, z):
        n = level_extent(level)
        if y < 0:
            return yl[pl.ds(y_row(level, x, z), 1)]
        if y >= n:
            return yh[pl.ds(y_row(level, x, z), 1)]
        if z < 0:
            return zl[pl.ds(z_row(level, x, y), 1)]
        if z >= n:
            return zh[pl.ds(z_row(level, x, y), 1)]
        return own_ref[pl.ds(own_row(level, x, y, z), 1)]

    for level in (6, 5, 4):
        n = level_extent(level)
        for z in range(-1, n + 1):
            for y in range(-1, n + 1):
                low, high = get(level, 0, y, z), get(level, n - 1, y, z)
                i = x_row(level, y, z)
                pa_ref[pl.ds(i, 1)] = jnp.where(odd, low, high)
                pb_ref[pl.ds(i, 1)] = jnp.where(odd, high, low)


def final_kernel(
    ids_ref, own_ref, za_ref, zb_ref, ya_ref, yb_ref, xa_ref, xb_ref, coarse_ref, occ_ref,
    coarse_sel_ref, near_ref, far_ref, spread_ref, basis_ref, back_ref, up_ref, down_ref,
    out_ref, src, wide,
):
    def put(base, values):
        high, low = split(values)
        src[base : base + values.shape[0], :512] = high
        src[base : base + values.shape[0], 512:] = low

    put(0, own_ref[...])
    stages = (
        (2, Z_BASE, Z_ROWS, za_ref, zb_ref),
        (1, Y_BASE, Y_ROWS, ya_ref, yb_ref),
        (0, X_BASE, X_ROWS, xa_ref, xb_ref),
    )
    for axis, base, rows, ra_ref, rb_ref in stages:
        odd = ids_ref[axis] == 1
        a, b = ra_ref[...], rb_ref[...]
        put(base, jnp.concatenate([jnp.where(odd, a, b), jnp.where(odd, b, a)], axis=0))
    src[336:SOURCES] = jnp.zeros((SOURCES - 336, 1024), BF16)

    three = coarse_ref[...]
    two = up_group(three, up_ref[...])
    wide_rows = jnp.concatenate([three, two, jnp.zeros((56, 512), F32)], axis=0)
    coarse_src = jnp.concatenate(split(times_exact(wide_rows, basis_ref[...])), axis=1)
    coarse_mix = mm(coarse_sel_ref[0], coarse_src)
    coarse_mix = coarse_mix[:, :512] + coarse_mix[:, 512:]

    for k, (_, ky, kz) in enumerate(KINDS):
        mix = mm(near_ref[ROWS * k : ROWS * k + ROWS], src[...])
        mix = mix[:, :512] + mix[:, 512:]
        mix = jnp.concatenate([mix[:72], mix[72:] + coarse_mix[8 * k : 8 * k + 8]], axis=0)
        high, low = split(mix)
        for t in range(4):
            c = source_class(t, ky, kz)
            wide[t, :ROWS, 128 * k : 128 * k + 128] = high[:, 128 * c : 128 * c + 128]
            wide[t, ROWS:, 128 * k : 128 * k + 128] = low[:, 128 * c : 128 * c + 128]
    parts = []
    for t in range(4):
        product = mm(wide[t], far_ref[t])
        parts.append(
            product[:ROWS, :128] + product[ROWS:, :128] + product[:ROWS, 128:] + product[ROWS:, 128:]
        )
    far = times_exact(jnp.concatenate(parts, axis=1), back_ref[...])

    lane = lax.broadcasted_iota(jnp.int32, (8, 512), 1) // 64
    down = down_ref[...]

    def only(row, octant):
        return jnp.where(lane == octant, jnp.broadcast_to(row, (8, 512)), 0.0)

    local = far[73:74] + times_pair(only(far[74:75], ids_ref[4]), down)
    local = far[72:73] + times_pair(only(local[:1], ids_ref[5]), down)
    local = far[64:72] + times_pair(jnp.broadcast_to(local[:1], (8, 512)) * octant_mask(8, 0), down)
    local = jnp.broadcast_to(local[:, None, :], (8, 8, 512)).reshape(64, 512) * octant_mask(64, 0)
    local = far[:64] + times_pair(local, down)
    out_ref[...] = local * occupancy_mask(occ_ref, spread_ref)


def pairs(axis, outer):
    result = []
    for i in range(512):
        c = place(i, 3)
        c[axis] = (c[axis] ^ 1) if not outer else c[axis] + (1 if c[axis] % 2 else -1)
        if 0 <= c[axis] < 8:
            result.append((i, morton(*c, 3)))
    return result


def exchange(pa, pb, axis):
    return lax.ppermute(pa, "d", pairs(axis, False)), lax.ppermute(pb, "d", pairs(axis, True))


SMEM = pl.BlockSpec(memory_space=pltpu.SMEM)
VMEM = pl.BlockSpec(memory_space=pltpu.VMEM)


def call(kernel, shapes, scratch, *args):
    return pl.pallas_call(
        kernel,
        out_shape=[jax.ShapeDtypeStruct(shape, F32) for shape in shapes],
        in_specs=[SMEM] + [VMEM] * (len(args) - 1),
        out_specs=[VMEM] * len(shapes),
        scratch_shapes=[pltpu.VMEM(shape, F32) for shape in scratch],
        compiler_params=pltpu.CompilerParams(vmem_limit_bytes=48 * 2**20),
    )(*args)


def local(multipoles, occupancy):
    const = {name: jnp.asarray(value) for name, value in constants().items()}
    me = lax.axis_index("d")
    parent = me // 8
    ids = jnp.stack([me % 2, me // 2 % 2, me // 4 % 2, parent, parent % 8, me % 8]).astype(jnp.int32)
    occ = occupancy.reshape(1, 512)
    own, pa, pb, three = call(
        upward_kernel,
        [(ROWS, 512), (Z_ROWS, 512), (Z_ROWS, 512), (8, 128)],
        [],
        ids, multipoles, occ, const["spread"], const["basis"], const["up"],
    )
    za, zb = exchange(pa, pb, 2)
    spread_three = jnp.broadcast_to(three[:1, :64], (512, 64))
    coarse = lax.all_to_all(spread_three, "d", 0, 0, tiled=True).reshape(64, 512)
    pa, pb = call(y_kernel, [(Y_ROWS, 512)] * 2, [(Z_ROWS, 512)] * 2, ids, own, za, zb)
    ya, yb = exchange(pa, pb, 1)
    pa, pb = call(
        x_kernel, [(X_ROWS, 512)] * 2, [(Z_ROWS, 512)] * 2 + [(Y_ROWS, 512)] * 2,
        ids, own, za, zb, ya, yb,
    )
    xa, xb = exchange(pa, pb, 0)
    whole = [own, za, zb, ya, yb, xa, xb, coarse, occ]
    tables = [const[name] for name in ("near", "far", "spread", "basis", "back", "up", "down")]
    full = lambda a: pl.BlockSpec(a.shape, lambda i, s, r=a.ndim: (0,) * r)
    return pl.pallas_call(
        final_kernel,
        out_shape=jax.ShapeDtypeStruct((64, 512), F32),
        grid_spec=pltpu.PrefetchScalarGridSpec(
            num_scalar_prefetch=1,
            grid=(1,),
            in_specs=[full(a) for a in whole]
            + [pl.BlockSpec((1, 216, 128), lambda i, s: (s[3], 0, 0))]
            + [full(a) for a in tables],
            out_specs=pl.BlockSpec((64, 512), lambda i, s: (0, 0)),
            scratch_shapes=[
                pltpu.VMEM((SOURCES, 1024), BF16),
                pltpu.VMEM((4, 2 * ROWS, 27 * 128), BF16),
            ],
        ),
        compiler_params=pltpu.CompilerParams(vmem_limit_bytes=52 * 2**20),
    )(ids, *whole, const["coarse"], *tables)


def solution(mesh):
    line = Mesh(mesh.devices.reshape(-1), ("d",))
    return jax.shard_map(
        local,
        mesh=line,
        in_specs=(P("d", None), P("d")),
        out_specs=P("d", None),
        check_vma=False,
    )
```

```python
import functools

import jax
import jax.numpy as jnp
import ml_dtypes
import numpy as np
from jax import lax
from jax.experimental import pallas as pl
from jax.experimental.pallas import tpu as pltpu
from jax.sharding import Mesh
from jax.sharding import PartitionSpec as P

F32 = jnp.float32
BF16 = jnp.bfloat16
NODES = np.cos((2.0 * np.arange(4) + 1.0) * (np.pi / 8.0))
ENTRY = np.arange(512)
OCT = [ENTRY // 64 % 2, ENTRY // 128 % 2, ENTRY // 256 % 2]
DEG = [ENTRY // 16 % 4, ENTRY // 4 % 4, ENTRY % 4]
KINDS = [(dx, ky, kz) for dx in (-1, 0, 1) for ky in range(3) for kz in range(3)]
ROWS = 80
SMALL = 16
PIECES = {
    "up": 512, "basis": 1024, "small": 432, "fine": 1728, "far": 13824, "back": 1024, "down": 512,
    "coarse": 64 * 224,
}


def halves(values):
    high = values.astype(np.float32).astype(ml_dtypes.bfloat16)
    low = (values - high.astype(np.float64)).astype(ml_dtypes.bfloat16)
    return high, low


def table(shift):
    distance = np.zeros((512, 512))
    reach = np.zeros((512, 512), int)
    for d in range(3):
        offset = 2 * shift[d] + OCT[d][:, None] - OCT[d][None, :]
        reach = np.maximum(reach, abs(offset))
        placed = NODES[DEG[d]]
        distance += (offset + 0.5 * (placed[:, None] - placed[None, :])) ** 2
    keep = reach >= 2
    return np.where(keep, 1.0 / np.sqrt(np.where(keep, distance, 1.0)), 0.0)


def upward_matrix():
    def terms(v):
        return [v, 2 * v * v - 1, 4 * v**3 - 3 * v]

    parent = np.arange(64)
    degrees = [parent // 16, parent // 4 % 4, parent % 4]
    result = np.ones((512, 64))
    for d in range(3):
        child = (OCT[d] - 0.5 + 0.5 * NODES[DEG[d]])[:, None]
        place = NODES[degrees[d]][None, :]
        result *= 0.25 + 0.5 * sum(a * b for a, b in zip(terms(place), terms(child)))
    return result


def parity_basis():
    basis = np.zeros((512, 512))
    for q in range(512):
        cy, cz = q // 128 % 2, q // 256
        ox, a, vy, vz = q // 64 % 2, q // 16 % 4, q // 4 % 4, q % 4
        for oy in range(2):
            for oz in range(2):
                b = 3 - vy if oy else vy
                e = 3 - vz if oz else vz
                sign = (-1) ** (cy * oy + cz * oz)
                basis[64 * (ox + 2 * oy + 4 * oz) + 16 * a + 4 * b + e, q] = 0.5 * sign
    return basis


def morton(x, y, z, bits):
    return sum(
        (x >> i & 1) << 3 * i | (y >> i & 1) << 3 * i + 1 | (z >> i & 1) << 3 * i + 2
        for i in range(bits)
    )


def place(number, bits):
    return [sum((number >> 3 * i + d & 1) << i for i in range(bits)) for d in range(3)]


Z_ROWS, Y_ROWS, X_ROWS = 24, 40, 64
Z_THREE, Y_THREE = 21, 35
FINE_PARTS = ((0, 64), (0, 16), (0, 16), (0, 24), (0, 24), (0, 40), (0, 40))
SMALL_PARTS = ((64, 80), (16, 24), (16, 24), (24, 40), (24, 40), (32, 64), (32, 64))


def level_extent(level):
    return 2 ** (level - 4)


def own_row(level, x, y, z):
    return {6: 0, 5: 64, 4: 72}[level] + morton(x, y, z, level - 4)


def z_row(level, x, y):
    n = level_extent(level)
    return {6: 0, 5: 16, 4: 20}[level] + y * n + x


def y_row(level, x, z):
    n = level_extent(level)
    return {6: 0, 5: 24, 4: 32}[level] + (z + 1) * n + x


def x_row(level, y, z):
    n = level_extent(level) + 2
    return {6: 0, 5: 36, 4: 52}[level] + (z + 1) * n + y + 1


def source_row(level, x, y, z):
    n = level_extent(level)
    if not 0 <= x < n:
        part, row = (6 if x >= n else 5), x_row(level, y, z)
    elif not 0 <= y < n:
        part, row = (4 if y >= n else 3), y_row(level, x, z)
    elif not 0 <= z < n:
        part, row = (2 if z >= n else 1), z_row(level, x, y)
    else:
        part, row = 0, own_row(level, x, y, z)
    parts = FINE_PARTS if level == 6 else SMALL_PARTS
    start, stop = parts[part]
    assert start <= row < stop
    return sum(q - p for p, q in parts[:part]) + row - start


def kind_terms(kind):
    return [(0, 1)] if kind == 0 else [(1, 1), (-1, 1 if kind == 1 else -1)]


def selections():
    fine = np.zeros((27, 64, 256))
    small = np.zeros((27, SMALL, 128))
    for k, (dx, ky, kz) in enumerate(KINDS):
        for dy, sy in kind_terms(ky):
            for dz, sz in kind_terms(kz):
                for level in (6, 5, 4):
                    n = level_extent(level)
                    into = fine[k] if level == 6 else small[k]
                    for m in range(n**3):
                        x, y, z = place(m, level - 4)
                        row = own_row(level, x, y, z) % 64
                        into[row, source_row(level, x + dx, y + dy, z + dz)] += (
                            sy * sz * 2.0 ** (level - 6)
                        )
    coarse = np.zeros((64, 27, SMALL, 128))
    for parent in range(64):
        for level, row, base in ((3, 9, 0), (2, 10, 64)):
            bits = level - 1
            n = 2**bits
            x, y, z = place(parent >> 3 * (2 - bits), bits)
            for k, (dx, ky, kz) in enumerate(KINDS):
                for dy, sy in kind_terms(ky):
                    for dz, sz in kind_terms(kz):
                        u = (x + dx, y + dy, z + dz)
                        if all(0 <= c < n for c in u):
                            coarse[parent, k, row, base + morton(*u, bits)] += (
                                sy * sz * 2.0 ** (level - 6)
                            )
    return (
        fine.reshape(27 * 64, 256).astype(ml_dtypes.bfloat16),
        small.reshape(27 * SMALL, 128).astype(ml_dtypes.bfloat16),
        np.concatenate(
            np.split(np.pad(coarse.reshape(64, 27 * SMALL, 128), ((0, 0), (0, 16), (0, 0))), 2, axis=1),
            axis=2,
        ).reshape(64 * 224, 256),
    )


@functools.lru_cache(maxsize=1)
def constants():
    basis = parity_basis()
    tables = {
        (dx, dy, dz): basis.T @ table((dx, dy, dz)) @ basis
        for dx in (-1, 0, 1)
        for dy in (0, 1)
        for dz in (0, 1)
    }
    far = np.zeros((4, 27 * 128, 256), ml_dtypes.bfloat16)
    for t in range(4):
        for k, (dx, ky, kz) in enumerate(KINDS):
            c = source_class(t, ky, kz)
            block = tables[dx, min(ky, 1), min(kz, 1)][
                128 * c : 128 * c + 128, 128 * t : 128 * t + 128
            ]
            high, low = halves(block)
            far[t, 128 * k : 128 * k + 128, :128] = high
            far[t, 128 * k : 128 * k + 128, 128:] = low
    up = upward_matrix()
    fine, small, coarse = selections()
    wide_down = np.concatenate(halves(np.tile(up.T, (2, 1))), axis=1)
    pieces = {
        "up": np.concatenate(halves(np.tile(up, (1, 2))), axis=1),
        "basis": in_lanes(basis),
        "small": np.pad(small, ((0, 0), (0, 128))),
        "fine": fine,
        "far": far.reshape(-1, 256),
        "back": in_lanes(basis.T),
        "down": in_lanes(wide_down),
        "coarse": coarse,
    }
    assert {name: len(piece) for name, piece in pieces.items()} == PIECES
    return np.concatenate([piece.astype(ml_dtypes.bfloat16) for piece in pieces.values()])


def in_lanes(matrix):
    return np.concatenate(np.split(matrix, matrix.shape[1] // 256, axis=1))


def source_class(t, ky, kz):
    return t ^ ((ky == 2) | (kz == 2) << 1)


def split(values):
    high = values.astype(BF16)
    return high, (values - high.astype(F32)).astype(BF16)


def mm(a, b):
    return jnp.dot(a, b, preferred_element_type=F32)


def stacked(values):
    rows, width = values.shape
    if rows % 16:
        values = jnp.concatenate([values, jnp.zeros((16 - rows % 16, width), F32)], axis=0)
    return jnp.concatenate(split(values), axis=0)


def times_exact(values, matrix):
    product = mm(stacked(values), matrix)
    half = product.shape[0] // 2
    return (product[:half] + product[half:])[: values.shape[0]]


def times_pair(values, matrix):
    product = mm(stacked(values), matrix)
    half = product.shape[0] // 2
    width = product.shape[1] // 2
    total = product[:half, :width] + product[half:, :width] + product[:half, width:]
    return total[: values.shape[0]]


def exact_times(matrix, values):
    product = mm(matrix, jnp.concatenate(split(values), axis=1))
    width = values.shape[1]
    return product[:, :width] + product[:, width:]


def piece_copy(blob, name, ref, sem, part=0, parts=1):
    start = sum(list(PIECES.values())[: list(PIECES).index(name)])
    rows = PIECES[name] // parts
    source = blob.at[pl.ds(pl.multiple_of(start + part * rows, 16), rows)]
    target = ref if ref.shape[0] == rows else ref.at[pl.ds(part * rows, rows)]
    return pltpu.make_async_copy(source, target, sem)


def in_columns(ref):
    rows = ref.shape[0] // 2
    return jnp.concatenate([ref[:rows], ref[rows:]], axis=1)


def iota(shape, axis):
    return lax.broadcasted_iota(jnp.int32, shape, axis)


def octant_mask(rows):
    return (iota((rows, 512), 1) // 64 == iota((rows, 512), 0) % 8).astype(F32)


def occupancy_mask(occ):
    kept = jnp.where(
        iota((64, 512), 1) // 8 == iota((64, 512), 0), jnp.broadcast_to(occ.astype(F32), (64, 512)), 0.0
    )
    spread = iota((512, 512), 0) % 8 == iota((512, 512), 1) // 64
    return mm(kept.astype(BF16), jnp.where(spread, 1.0, 0.0).astype(BF16))


def upward(values, up):
    twice = times_pair(values, up)
    return jnp.concatenate([twice] * 4, axis=1)


def up_group(values, up):
    rows = values.shape[0]
    return (upward(values, up) * octant_mask(rows)).reshape(rows // 8, 8, 512).sum(axis=1)


def downward(masked, down):
    folded = masked[:, :128] + masked[:, 128:256] + masked[:, 256:384] + masked[:, 384:]
    return times_pair(folded, down)


def upward_kernel(
    ids_ref, mult_hbm, occ_hbm, blob, own_ref, pa_ref, pb_ref, mask_ref,
    mult_ref, occ_ref, up_ref, basis_ref, sem,
):
    copies = [
        pltpu.make_async_copy(occ_hbm, occ_ref, sem.at[0]),
        pltpu.make_async_copy(mult_hbm, mult_ref, sem.at[1]),
        piece_copy(blob, "up", up_ref, sem.at[2]),
        piece_copy(blob, "basis", basis_ref, sem.at[3]),
    ]
    for copy in copies:
        copy.start()
    copies[0].wait()
    mask_ref[...] = occupancy_mask(occ_ref[...])
    copies[1].wait()
    copies[2].wait()
    grouped_six = mult_ref[...] * mask_ref[...]
    grouped_five = up_group(grouped_six, up_ref[...])
    grouped_four = up_group(grouped_five, up_ref[...])
    three = upward(jnp.broadcast_to(grouped_four, (8, 512)), up_ref[...])
    copies[3].wait()
    basis = in_columns(basis_ref)
    own_ref[0:64] = times_exact(grouped_six, basis)
    rest = jnp.concatenate([grouped_five, jnp.broadcast_to(grouped_four, (8, 512))], axis=0)
    own_ref[64:80] = times_exact(rest, basis)
    odd = ids_ref[2] == 1
    for p_ref in (pa_ref, pb_ref):
        p_ref[Z_ROWS - 8 :] = three
    for level in (6, 5, 4):
        n = level_extent(level)
        for y in range(n):
            for x in range(n):
                low = own_ref[pl.ds(own_row(level, x, y, 0), 1)]
                high = own_ref[pl.ds(own_row(level, x, y, n - 1), 1)]
                i = z_row(level, x, y)
                pa_ref[pl.ds(i, 1)] = jnp.where(odd, low, high)
                pb_ref[pl.ds(i, 1)] = jnp.where(odd, high, low)


def sort_sides(odd, ra_ref, rb_ref, low_ref, high_ref):
    a, b = ra_ref[...], rb_ref[...]
    low_ref[...] = jnp.where(odd, a, b)
    high_ref[...] = jnp.where(odd, b, a)


def y_kernel(ids_ref, own_ref, sent_ref, za_ref, zb_ref, pa_ref, pb_ref, zl, zh):
    sort_sides(ids_ref[2] == 1, za_ref, zb_ref, zl, zh)
    odd = ids_ref[1] == 1
    pa_ref[...] = jnp.zeros_like(pa_ref)
    pb_ref[...] = jnp.zeros_like(pb_ref)
    mine, other = sent_ref[pl.ds(Z_THREE, 1)], za_ref[pl.ds(Z_THREE, 1)]
    pa_ref[pl.ds(Y_THREE, 1)] = jnp.where(
        iota((1, 512), 1) // 128 % 2 == ids_ref[2], mine, other
    )

    def get(level, x, y, z):
        n = level_extent(level)
        if z < 0:
            return zl[pl.ds(z_row(level, x, y), 1)]
        if z >= n:
            return zh[pl.ds(z_row(level, x, y), 1)]
        return own_ref[pl.ds(own_row(level, x, y, z), 1)]

    for level in (6, 5, 4):
        n = level_extent(level)
        for z in range(-1, n + 1):
            for x in range(n):
                low, high = get(level, x, 0, z), get(level, x, n - 1, z)
                i = y_row(level, x, z)
                pa_ref[pl.ds(i, 1)] = jnp.where(odd, low, high)
                pb_ref[pl.ds(i, 1)] = jnp.where(odd, high, low)


def x_kernel(ids_ref, own_ref, za_ref, zb_ref, ya_ref, yb_ref, pa_ref, pb_ref, zl, zh, yl, yh):
    sort_sides(ids_ref[2] == 1, za_ref, zb_ref, zl, zh)
    sort_sides(ids_ref[1] == 1, ya_ref, yb_ref, yl, yh)
    odd = ids_ref[0] == 1
    pa_ref[...] = jnp.zeros_like(pa_ref)
    pb_ref[...] = jnp.zeros_like(pb_ref)

    def get(level, x, y, z):
        n = level_extent(level)
        if y < 0:
            return yl[pl.ds(y_row(level, x, z), 1)]
        if y >= n:
            return yh[pl.ds(y_row(level, x, z), 1)]
        if z < 0:
            return zl[pl.ds(z_row(level, x, y), 1)]
        if z >= n:
            return zh[pl.ds(z_row(level, x, y), 1)]
        return own_ref[pl.ds(own_row(level, x, y, z), 1)]

    for level in (6, 5, 4):
        n = level_extent(level)
        for z in range(-1, n + 1):
            for y in range(-1, n + 1):
                low, high = get(level, 0, y, z), get(level, n - 1, y, z)
                i = x_row(level, y, z)
                pa_ref[pl.ds(i, 1)] = jnp.where(odd, low, high)
                pb_ref[pl.ds(i, 1)] = jnp.where(odd, high, low)


def coarse_rows(quads):
    half = iota((128, 128), 1) // 64
    keep = half == iota((128, 128), 0) % 2
    blocks = []
    for i in range(4):
        pair = quads[:, 128 * (i // 2) : 128 * (i // 2) + 128]
        both = jnp.where(half == i % 2, pair, pltpu.roll(pair, 64, 1))
        blocks.append(jnp.where(keep, both, 0.0))
    gather = jnp.where(iota((64, 128), 0) == iota((64, 128), 1) // 2, 1.0, 0.0).astype(BF16)
    return exact_times(gather, jnp.concatenate(blocks, axis=1))


def final_kernel(
    ids_ref, own_ref, za_ref, zb_ref, ya_ref, yb_ref, xa_ref, xb_ref, quads_ref, mask_ref, blob,
    out_ref, fine_src, small_src, wide, coarse_ref, up_ref, basis_ref, small_ref, fine_ref, far_ref,
    back_ref, down_ref, sem,
):
    small_copy = piece_copy(blob, "small", small_ref, sem.at[0])
    fine_copy = piece_copy(blob, "fine", fine_ref, sem.at[1])
    up_copy = piece_copy(blob, "up", up_ref, sem.at[2])
    basis_copy = piece_copy(blob, "basis", basis_ref, sem.at[3])
    coarse_copy = piece_copy(blob, "coarse", coarse_ref, sem.at[4], ids_ref[3], 64)
    far_copies = [piece_copy(blob, "far", far_ref, sem.at[5 + t], t, 4) for t in range(4)]
    back_copy = piece_copy(blob, "back", back_ref, sem.at[9])
    down_copy = piece_copy(blob, "down", down_ref, sem.at[10])
    first = (small_copy, up_copy, basis_copy, coarse_copy, fine_copy)
    for copy in (*first, *far_copies, back_copy, down_copy):
        copy.start()
    fine_src[224:] = jnp.zeros((32, 512), F32)
    stack = [own_ref[...]]
    for axis, ra_ref, rb_ref in ((2, za_ref, zb_ref), (1, ya_ref, yb_ref), (0, xa_ref, xb_ref)):
        odd = ids_ref[axis] == 1
        a, b = ra_ref[...], rb_ref[...]
        stack += [jnp.where(odd, a, b), jnp.where(odd, b, a)]
    for target, parts in ((fine_src, FINE_PARTS), (small_src, SMALL_PARTS)):
        base = 0
        for values, (start, stop) in zip(stack, parts):
            target[base : base + stop - start] = values[start:stop]
            base += stop - start

    small_copy.wait()
    small = exact_times(small_ref[:, :128], small_src[...])
    three = coarse_rows(quads_ref[...])
    up_copy.wait()
    two = up_group(three, up_ref[...])
    upper = jnp.concatenate([three, two, jnp.zeros((56, 512), F32)], axis=0)
    basis_copy.wait()
    upper = times_exact(upper, in_columns(basis_ref))
    coarse_copy.wait()
    chosen = jnp.concatenate([coarse_ref[:, :128], coarse_ref[:208, 128:]], axis=0)
    small = small + exact_times(chosen, upper)

    fine_split = jnp.concatenate(split(fine_src[...]), axis=1)
    fine_copy.wait()
    for group in range(3):
        mixes = mm(fine_ref[576 * group : 576 * group + 576], fine_split)
        mixes = mixes[:, :512] + mixes[:, 512:]
        for j in range(9):
            k = 9 * group + j
            _, ky, kz = KINDS[k]
            mix = jnp.concatenate(
                [mixes[64 * j : 64 * j + 64], small[SMALL * k : SMALL * k + SMALL]], axis=0
            )
            high, low = split(mix)
            for t in range(4):
                c = source_class(t, ky, kz)
                wide[t, :ROWS, 128 * k : 128 * k + 128] = high[:, 128 * c : 128 * c + 128]
                wide[t, ROWS:, 128 * k : 128 * k + 128] = low[:, 128 * c : 128 * c + 128]
    parts = []
    for t in range(4):
        far_copies[t].wait()
        product = mm(wide[t], far_ref[3456 * t : 3456 * t + 3456])
        parts.append(
            product[:ROWS, :128] + product[ROWS:, :128] + product[:ROWS, 128:] + product[ROWS:, 128:]
        )
    back_copy.wait()
    far = times_exact(jnp.concatenate(parts, axis=1), in_columns(back_ref))
    down_copy.wait()

    lane = iota((8, 512), 1) // 64
    down = jnp.concatenate([down_ref[128 * i : 128 * i + 128] for i in range(4)], axis=1)

    def only(row, octant):
        return jnp.where(lane == octant, jnp.broadcast_to(row, (8, 512)), 0.0)

    local = far[73:74] + downward(only(far[74:75], ids_ref[4]), down)
    local = far[72:73] + downward(only(local[:1], ids_ref[5]), down)
    local = far[64:72] + downward(jnp.broadcast_to(local[:1], (8, 512)) * octant_mask(8), down)
    local = jnp.broadcast_to(local[:, None, :], (8, 8, 512)).reshape(64, 512) * octant_mask(64)
    out_ref[...] = (far[:64] + downward(local, down)) * mask_ref[...]


def pairs(axis, outer):
    result = []
    for i in range(512):
        c = place(i, 3)
        c[axis] = (c[axis] ^ 1) if not outer else c[axis] + (1 if c[axis] % 2 else -1)
        if 0 <= c[axis] < 8:
            result.append((i, morton(*c, 3)))
    return result


def exchange(pa, pb, axis):
    return (
        lax.ppermute(pa, AXES, pairs(axis, False)),
        lax.ppermute(pb, AXES, pairs(axis, True)),
    )


SMEM = pl.BlockSpec(memory_space=pltpu.SMEM)
VMEM = pl.BlockSpec(memory_space=pltpu.VMEM)
HBM = pl.BlockSpec(memory_space=pltpu.HBM)
AXES = ("upper", "bit2", "bit1", "bit0")
LIMIT = 52 * 2**20


def call(kernel, shapes, scratch, ids, vmem_args, hbm_args=(), micros=1):
    return pl.pallas_call(
        kernel,
        out_shape=[jax.ShapeDtypeStruct(shape, F32) for shape in shapes],
        in_specs=[SMEM] + [VMEM] * len(vmem_args) + [HBM] * len(hbm_args),
        out_specs=[VMEM] * len(shapes),
        scratch_shapes=scratch,
        compiler_params=pltpu.CompilerParams(vmem_limit_bytes=LIMIT),
        cost_estimate=pl.CostEstimate(flops=micros * 10**9, bytes_accessed=0, transcendentals=0),
    )(ids, *vmem_args, *hbm_args)


def rows_of(*counts):
    return [(count, 512) for count in counts]


def scratch_rows(*counts):
    return [pltpu.VMEM((count, 512), F32) for count in counts]


def table_scratch(*names):
    return [pltpu.VMEM((PIECES[name], 256), BF16) for name in names]


def local(multipoles, occupancy):
    blob = jnp.asarray(constants())
    me = lax.axis_index(AXES)
    parent = me // 8
    ids = jnp.stack([me % 2, me // 2 % 2, me // 4 % 2, parent, parent % 8, me % 8]).astype(jnp.int32)
    own, pa, pb, mask = call(
        upward_kernel,
        rows_of(ROWS, Z_ROWS, Z_ROWS, 64),
        scratch_rows(64)
        + [pltpu.VMEM((1, 512), jnp.int32)]
        + table_scratch("up", "basis")
        + [pltpu.SemaphoreType.DMA((4,))],
        ids, [], [multipoles, occupancy.reshape(1, 512), blob], micros=4,
    )
    za, zb = exchange(pa, pb, 2)
    pa, pb = call(
        y_kernel, rows_of(Y_ROWS, Y_ROWS), scratch_rows(Z_ROWS, Z_ROWS), ids, [own, pa, za, zb]
    )
    ya, yb = exchange(pa, pb, 1)
    ours, theirs = (p[Y_THREE : Y_THREE + 1, :256] for p in (pa, ya))
    quad = jnp.where(jnp.arange(256)[None] // 64 % 2 == ids[1], ours, theirs)
    quads = lax.all_to_all(
        jnp.broadcast_to(quad, (128, 256)), ("upper", "bit0"), 0, 0, tiled=True
    )
    pa, pb = call(
        x_kernel, rows_of(X_ROWS, X_ROWS), scratch_rows(Z_ROWS, Z_ROWS, Y_ROWS, Y_ROWS),
        ids, [own, za, zb, ya, yb], micros=40,
    )
    xa, xb = exchange(pa, pb, 0)
    (out,) = call(
        final_kernel,
        rows_of(64),
        scratch_rows(256, 128)
        + [pltpu.VMEM((4, 2 * ROWS, 27 * 128), BF16), pltpu.VMEM((224, 256), BF16)]
        + table_scratch(*list(PIECES)[:-1])
        + [pltpu.SemaphoreType.DMA((11,))],
        ids, [own, za, zb, ya, yb, xa, xb, quads, mask], [blob], micros=8,
    )
    return out


def solution(mesh):
    fine_mesh = Mesh(mesh.devices.reshape(64, 2, 2, 2), AXES)
    return jax.shard_map(
        local,
        mesh=fine_mesh,
        in_specs=(P(AXES, None), P(AXES)),
        out_specs=P(AXES, None),
        check_vma=False,
    )
```

```python
import functools

import jax
import jax.numpy as jnp
import ml_dtypes
import numpy as np
from jax import lax
from jax.experimental import pallas as pl
from jax.experimental.pallas import tpu as pltpu
from jax.sharding import Mesh
from jax.sharding import PartitionSpec as P

F32 = jnp.float32
BF16 = jnp.bfloat16
NODES = np.cos((2.0 * np.arange(4) + 1.0) * (np.pi / 8.0))
ENTRY = np.arange(512)
OCT = [ENTRY // 64 % 2, ENTRY // 128 % 2, ENTRY // 256 % 2]
DEG = [ENTRY // 16 % 4, ENTRY // 4 % 4, ENTRY % 4]
KINDS = [(dx, ky, kz) for dx in (-1, 0, 1) for ky in range(3) for kz in range(3)]
ROWS = 80
SMALL = 16
PIECES = {
    "up": 512, "basis": 1024, "small": 432, "fine": 1728, "rim": 288, "spot": 80, "far": 9216,
    "back": 1024, "down": 512, "coarse": 64 * 224,
}


def halves(values):
    high = values.astype(np.float32).astype(ml_dtypes.bfloat16)
    low = (values - high.astype(np.float64)).astype(ml_dtypes.bfloat16)
    return high, low


def table(shift):
    distance = np.zeros((512, 512))
    reach = np.zeros((512, 512), int)
    for d in range(3):
        offset = 2 * shift[d] + OCT[d][:, None] - OCT[d][None, :]
        reach = np.maximum(reach, abs(offset))
        placed = NODES[DEG[d]]
        distance += (offset + 0.5 * (placed[:, None] - placed[None, :])) ** 2
    keep = reach >= 2
    return np.where(keep, 1.0 / np.sqrt(np.where(keep, distance, 1.0)), 0.0)


def upward_matrix():
    def terms(v):
        return [v, 2 * v * v - 1, 4 * v**3 - 3 * v]

    parent = np.arange(64)
    degrees = [parent // 16, parent // 4 % 4, parent % 4]
    result = np.ones((512, 64))
    for d in range(3):
        child = (OCT[d] - 0.5 + 0.5 * NODES[DEG[d]])[:, None]
        place = NODES[degrees[d]][None, :]
        result *= 0.25 + 0.5 * sum(a * b for a, b in zip(terms(place), terms(child)))
    return result


def parity_signs():
    signs = np.zeros((512, 512))
    for q in range(512):
        odd = [q // 64 % 2, q // 128 % 2, q // 256]
        degree = [q // 16 % 4, q // 4 % 4, q % 4]
        for o in range(8):
            octant = [o % 2, o // 2 % 2, o // 4]
            a, b, e = (3 - v if side else v for v, side in zip(degree, octant))
            sign = (-1) ** sum(c * side for c, side in zip(odd, octant))
            signs[64 * o + 16 * a + 4 * b + e, q] = sign
    return signs


def morton(x, y, z, bits):
    return sum(
        (x >> i & 1) << 3 * i | (y >> i & 1) << 3 * i + 1 | (z >> i & 1) << 3 * i + 2
        for i in range(bits)
    )


def place(number, bits):
    return [sum((number >> 3 * i + d & 1) << i for i in range(bits)) for d in range(3)]


Z_ROWS, Y_ROWS, X_ROWS = 24, 40, 64
Z_THREE, Y_THREE = 21, 35
FINE_PARTS = ((0, 64), (0, 16), (0, 16), (0, 24), (0, 24))
SMALL_PARTS = ((64, 80), (16, 24), (16, 24), (24, 40), (24, 40))
RIM = 32


def level_extent(level):
    return 2 ** (level - 4)


def own_row(level, x, y, z):
    return {6: 0, 5: 64, 4: 72}[level] + morton(x, y, z, level - 4)


def z_row(level, x, y):
    n = level_extent(level)
    return {6: 0, 5: 16, 4: 20}[level] + y * n + x


def y_row(level, x, z):
    n = level_extent(level)
    return {6: 0, 5: 24, 4: 32}[level] + (z + 1) * n + x


def x_row(level, y, z):
    n = level_extent(level) + 2
    return {6: 0, 5: 36, 4: 52}[level] + (z + 1) * n + y + 1


def source_row(level, x, y, z):
    n = level_extent(level)
    if not 0 <= y < n:
        part, row = (4 if y >= n else 3), y_row(level, x, z)
    elif not 0 <= z < n:
        part, row = (2 if z >= n else 1), z_row(level, x, y)
    else:
        part, row = 0, own_row(level, x, y, z)
    parts = FINE_PARTS if level == 6 else SMALL_PARTS
    start, stop = parts[part]
    assert start <= row < stop
    return sum(q - p for p, q in parts[:part]) + row - start


def kind_terms(kind):
    return [(0, 1)] if kind == 0 else [(1, 1), (-1, 1 if kind == 1 else -1)]


def rim_target(level, y, z):
    return {6: 0, 5: 16, 4: 20}[level] + z * level_extent(level) + y


def selections():
    fine = np.zeros((27, 64, 256))
    small = np.zeros((27, SMALL, 128))
    rim = np.zeros((9, RIM, 256))
    spot = np.zeros((ROWS, 256))
    for k, (dx, ky, kz) in enumerate(KINDS):
        for dy, sy in kind_terms(ky):
            for dz, sz in kind_terms(kz):
                for level in (6, 5, 4):
                    n = level_extent(level)
                    factor = sy * sz * 2.0 ** (level - 6)
                    into = fine[k] if level == 6 else small[k]
                    for m in range(n**3):
                        x, y, z = place(m, level - 4)
                        row = own_row(level, x, y, z) % 64
                        if 0 <= x + dx < n:
                            into[row, source_row(level, x + dx, y + dy, z + dz)] += factor
                        elif dx == 1:
                            rim[k - 18, rim_target(level, y, z), x_row(level, y + dy, z + dz)] += factor
                            spot[own_row(level, x, y, z), rim_target(level, y, z)] = 1
                        else:
                            spot[own_row(level, x, y, z), RIM + rim_target(level, y, z)] = 1
    coarse = np.zeros((64, 27, SMALL, 128))
    for parent in range(64):
        for level, row, base in ((3, 9, 0), (2, 10, 64)):
            bits = level - 1
            n = 2**bits
            x, y, z = place(parent >> 3 * (2 - bits), bits)
            for k, (dx, ky, kz) in enumerate(KINDS):
                for dy, sy in kind_terms(ky):
                    for dz, sz in kind_terms(kz):
                        u = (x + dx, y + dy, z + dz)
                        if all(0 <= c < n for c in u):
                            coarse[parent, k, row, base + morton(*u, bits)] += (
                                sy * sz * 2.0 ** (level - 6)
                            )
    coarse = np.pad(coarse.reshape(64, 27 * SMALL, 128), ((0, 0), (0, 16), (0, 0)))
    return {
        "small": np.pad(small.reshape(27 * SMALL, 128), ((0, 0), (0, 128))),
        "fine": fine.reshape(27 * 64, 256),
        "rim": rim.reshape(9 * RIM, 256),
        "spot": spot,
        "coarse": np.concatenate(np.split(coarse, 2, axis=1), axis=2).reshape(64 * 224, 256),
    }


@functools.lru_cache(maxsize=1)
def constants():
    basis, back = 0.5 * parity_signs(), 0.25 * parity_signs().T
    tables = {
        (dx, dy, dz): back @ table((dx, dy, dz)) @ basis
        for dx in (0, 1)
        for dy in (0, 1)
        for dz in (0, 1)
    }
    far = np.zeros((2, 4, 9 * 128, 256), ml_dtypes.bfloat16)
    for t in range(4):
        for k, (dx, ky, kz) in enumerate(KINDS[9:]):
            c = source_class(t, ky, kz)
            block = tables[dx, min(ky, 1), min(kz, 1)][
                128 * c : 128 * c + 128, 128 * t : 128 * t + 128
            ]
            high, low = halves(block)
            j = 128 * (k % 9)
            far[dx, t, j : j + 128, :128] = high
            far[dx, t, j : j + 128, 128:] = low
    up = upward_matrix()
    wide_down = np.concatenate(halves(np.tile(up.T, (2, 1))), axis=1)
    pieces = selections() | {
        "up": np.concatenate(halves(np.tile(up, (1, 2))), axis=1),
        "basis": in_lanes(basis),
        "far": far.reshape(-1, 256),
        "back": in_lanes(back),
        "down": in_lanes(wide_down),
    }
    assert {name: len(piece) for name, piece in pieces.items()} == PIECES
    return np.concatenate([pieces[name].astype(ml_dtypes.bfloat16) for name in PIECES])


def in_lanes(matrix):
    return np.concatenate(np.split(matrix, matrix.shape[1] // 256, axis=1))


def source_class(t, ky, kz):
    return t ^ ((ky == 2) | (kz == 2) << 1)


def split(values):
    high = values.astype(BF16)
    return high, (values - high.astype(F32)).astype(BF16)


def mm(a, b):
    return jnp.dot(a, b, preferred_element_type=F32)


def stacked(values):
    rows, width = values.shape
    if rows % 16:
        values = jnp.concatenate([values, jnp.zeros((16 - rows % 16, width), F32)], axis=0)
    return jnp.concatenate(split(values), axis=0)


def times_exact(values, matrix):
    product = mm(stacked(values), matrix)
    half = product.shape[0] // 2
    return (product[:half] + product[half:])[: values.shape[0]]


def times_pair(values, matrix):
    product = mm(stacked(values), matrix)
    half = product.shape[0] // 2
    width = product.shape[1] // 2
    total = product[:half, :width] + product[half:, :width] + product[:half, width:]
    return total[: values.shape[0]]


def exact_times(matrix, values):
    product = mm(matrix, jnp.concatenate(split(values), axis=1))
    width = values.shape[1]
    return product[:, :width] + product[:, width:]


def piece_copy(blob, name, ref, sem, part=0, parts=1):
    start = sum(list(PIECES.values())[: list(PIECES).index(name)])
    rows = PIECES[name] // parts
    source = blob.at[pl.ds(pl.multiple_of(start + part * rows, 16), rows)]
    target = ref if ref.shape[0] == rows else ref.at[pl.ds(part * rows, rows)]
    return pltpu.make_async_copy(source, target, sem)


def in_columns(ref):
    rows = ref.shape[0] // 2
    return jnp.concatenate([ref[:rows], ref[rows:]], axis=1)


def iota(shape, axis):
    return lax.broadcasted_iota(jnp.int32, shape, axis)


def octant_mask(rows):
    return (iota((rows, 512), 1) // 64 == iota((rows, 512), 0) % 8).astype(F32)


def occupancy_mask(occ):
    kept = jnp.where(
        iota((64, 512), 1) // 8 == iota((64, 512), 0), jnp.broadcast_to(occ.astype(F32), (64, 512)), 0.0
    )
    spread = iota((512, 512), 0) % 8 == iota((512, 512), 1) // 64
    return mm(kept.astype(BF16), jnp.where(spread, 1.0, 0.0).astype(BF16))


def upward(values, up):
    twice = times_pair(values, up)
    return jnp.concatenate([twice] * 4, axis=1)


def up_group(values, up):
    rows = values.shape[0]
    return (upward(values, up) * octant_mask(rows)).reshape(rows // 8, 8, 512).sum(axis=1)


def downward(masked, down):
    folded = masked[:, :128] + masked[:, 128:256] + masked[:, 256:384] + masked[:, 384:]
    return times_pair(folded, down)


def upward_kernel(
    ids_ref, mult_hbm, occ_hbm, blob, own_ref, pa_ref, pb_ref, mask_ref,
    mult_ref, occ_ref, up_ref, basis_ref, sem,
):
    copies = [
        pltpu.make_async_copy(occ_hbm, occ_ref, sem.at[0]),
        pltpu.make_async_copy(mult_hbm, mult_ref, sem.at[1]),
        piece_copy(blob, "up", up_ref, sem.at[2]),
        piece_copy(blob, "basis", basis_ref, sem.at[3]),
    ]
    for copy in copies:
        copy.start()
    copies[0].wait()
    mask_ref[...] = occupancy_mask(occ_ref[...])
    copies[1].wait()
    copies[2].wait()
    grouped_six = mult_ref[...] * mask_ref[...]
    grouped_five = up_group(grouped_six, up_ref[...])
    grouped_four = up_group(grouped_five, up_ref[...])
    three = upward(jnp.broadcast_to(grouped_four, (8, 512)), up_ref[...])
    copies[3].wait()
    basis = in_columns(basis_ref)
    own_ref[0:64] = times_exact(grouped_six, basis)
    rest = jnp.concatenate([grouped_five, jnp.broadcast_to(grouped_four, (8, 512))], axis=0)
    own_ref[64:80] = times_exact(rest, basis)
    odd = ids_ref[2] == 1
    for p_ref in (pa_ref, pb_ref):
        p_ref[Z_ROWS - 8 :] = three
    for level in (6, 5, 4):
        n = level_extent(level)
        for y in range(n):
            for x in range(n):
                low = own_ref[pl.ds(own_row(level, x, y, 0), 1)]
                high = own_ref[pl.ds(own_row(level, x, y, n - 1), 1)]
                i = z_row(level, x, y)
                pa_ref[pl.ds(i, 1)] = jnp.where(odd, low, high)
                pb_ref[pl.ds(i, 1)] = jnp.where(odd, high, low)


def sort_sides(odd, ra_ref, rb_ref, low_ref, high_ref):
    a, b = ra_ref[...], rb_ref[...]
    low_ref[...] = jnp.where(odd, a, b)
    high_ref[...] = jnp.where(odd, b, a)


def y_kernel(ids_ref, own_ref, sent_ref, zb_ref, za_ref, pa_ref, pb_ref, zl, zh):
    sort_sides(ids_ref[2] == 1, za_ref, zb_ref, zl, zh)
    odd = ids_ref[1] == 1
    pa_ref[...] = jnp.zeros_like(pa_ref)
    pb_ref[...] = jnp.zeros_like(pb_ref)
    mine, other = sent_ref[pl.ds(Z_THREE, 1)], za_ref[pl.ds(Z_THREE, 1)]
    pa_ref[pl.ds(Y_THREE, 1)] = jnp.where(
        iota((1, 512), 1) // 128 % 2 == ids_ref[2], mine, other
    )

    def get(level, x, y, z):
        n = level_extent(level)
        if z < 0:
            return zl[pl.ds(z_row(level, x, y), 1)]
        if z >= n:
            return zh[pl.ds(z_row(level, x, y), 1)]
        return own_ref[pl.ds(own_row(level, x, y, z), 1)]

    for level in (6, 5, 4):
        n = level_extent(level)
        for z in range(-1, n + 1):
            for x in range(n):
                low, high = get(level, x, 0, z), get(level, x, n - 1, z)
                i = y_row(level, x, z)
                pa_ref[pl.ds(i, 1)] = jnp.where(odd, low, high)
                pb_ref[pl.ds(i, 1)] = jnp.where(odd, high, low)


def x_kernel(ids_ref, own_ref, zb_ref, za_ref, ya_ref, yb_ref, pa_ref, pb_ref, zl, zh, yl, yh):
    sort_sides(ids_ref[2] == 1, za_ref, zb_ref, zl, zh)
    sort_sides(ids_ref[1] == 1, ya_ref, yb_ref, yl, yh)
    odd = ids_ref[0] == 1
    pa_ref[...] = jnp.zeros_like(pa_ref)
    pb_ref[...] = jnp.zeros_like(pb_ref)

    def get(level, x, y, z):
        n = level_extent(level)
        if y < 0:
            return yl[pl.ds(y_row(level, x, z), 1)]
        if y >= n:
            return yh[pl.ds(y_row(level, x, z), 1)]
        if z < 0:
            return zl[pl.ds(z_row(level, x, y), 1)]
        if z >= n:
            return zh[pl.ds(z_row(level, x, y), 1)]
        return own_ref[pl.ds(own_row(level, x, y, z), 1)]

    for level in (6, 5, 4):
        n = level_extent(level)
        for z in range(-1, n + 1):
            for y in range(-1, n + 1):
                low, high = get(level, 0, y, z), get(level, n - 1, y, z)
                i = x_row(level, y, z)
                pa_ref[pl.ds(i, 1)] = jnp.where(odd, low, high)
                pb_ref[pl.ds(i, 1)] = jnp.where(odd, high, low)


def coarse_rows(quads):
    half = iota((128, 128), 1) // 64
    keep = half == iota((128, 128), 0) % 2
    blocks = []
    for i in range(4):
        pair = quads[:, 128 * (i // 2) : 128 * (i // 2) + 128]
        both = jnp.where(half == i % 2, pair, pltpu.roll(pair, 64, 1))
        blocks.append(jnp.where(keep, both, 0.0))
    gather = jnp.where(iota((64, 128), 0) == iota((64, 128), 1) // 2, 1.0, 0.0).astype(BF16)
    return exact_times(gather, jnp.concatenate(blocks, axis=1))


def place_mix(wide, j, ky, kz, mix, row):
    rows, half = mix.shape[0], wide.shape[1] // 2
    high, low = split(mix)
    for t in range(4):
        c = source_class(t, ky, kz)
        wide[t, row : row + rows, 128 * j : 128 * j + 128] = high[:, 128 * c : 128 * c + 128]
        wide[t, half + row : half + row + rows, 128 * j : 128 * j + 128] = low[:, 128 * c : 128 * c + 128]


def far_rows(wide, far_ref, dx):
    parts = []
    for t in range(4):
        rows = 1152 * (4 * dx + t)
        product = mm(wide[t], far_ref[rows : rows + 1152])
        half = product.shape[0] // 2
        top, bottom = product[:half], product[half:]
        parts.append((top[:, :128] + bottom[:, :128]) + (top[:, 128:] + bottom[:, 128:]))
    return jnp.concatenate(parts, axis=1)


def reflected(rows):
    return jnp.where(iota(rows.shape, 1) // 64 % 2 == 1, -rows, rows)


def whole_down(down_ref):
    return jnp.concatenate([down_ref[128 * i : 128 * i + 128] for i in range(4)], axis=1)


def only(row, octant):
    kept = iota((8, 512), 1) // 64 == octant
    return jnp.where(kept, jnp.broadcast_to(row, (8, 512)), 0.0)


def inner_kernel(
    ids_ref, own_ref, zb_ref, za_ref, ya_ref, yb_ref, blob, out_ref,
    fine_src, small_src, wide_zero, wide_one, small_ref, fine_ref, far_ref, sem,
):
    small_copy = piece_copy(blob, "small", small_ref, sem.at[0])
    fine_copy = piece_copy(blob, "fine", fine_ref, sem.at[1])
    tables = [piece_copy(blob, "far", far_ref, sem.at[2 + dx], dx, 2) for dx in range(2)]
    for copy in (small_copy, fine_copy, *tables):
        copy.start()
    fine_src[144:] = jnp.zeros((112, 512), F32)
    small_src[64:] = jnp.zeros((64, 512), F32)
    stack = [own_ref[...]]
    for axis, ra_ref, rb_ref in ((2, za_ref, zb_ref), (1, ya_ref, yb_ref)):
        odd = ids_ref[axis] == 1
        a, b = ra_ref[...], rb_ref[...]
        stack += [jnp.where(odd, a, b), jnp.where(odd, b, a)]
    for target, parts in ((fine_src, FINE_PARTS), (small_src, SMALL_PARTS)):
        base = 0
        for values, (start, stop) in zip(stack, parts):
            target[base : base + stop - start] = values[start:stop]
            base += stop - start
    small_copy.wait()
    small = exact_times(small_ref[:, :128], small_src[...])
    fine_split = jnp.concatenate(split(fine_src[...]), axis=1)
    fine_copy.wait()
    far = 0.0
    for group in (1, 0, 2):
        mixes = mm(fine_ref[576 * group : 576 * group + 576], fine_split)
        mixes = mixes[:, :512] + mixes[:, 512:]
        for j in range(9):
            k = 9 * group + j
            _, ky, kz = KINDS[k]
            mix = [mixes[64 * j : 64 * j + 64], small[SMALL * k : SMALL * k + SMALL]]
            mix = jnp.concatenate(mix, axis=0)
            if group == 1:
                place_mix(wide_zero, j, ky, kz, mix, 0)
            else:
                mix = reflected(mix) if group == 0 else mix
                place_mix(wide_one, j, ky, kz, mix, ROWS if group == 0 else 0)
        if group == 1:
            tables[0].wait()
            far = far_rows(wide_zero, far_ref, 0)
    tables[1].wait()
    both = far_rows(wide_one, far_ref, 1)
    out_ref[...] = far + both[:ROWS] + reflected(both[ROWS:])


def outer_kernel(
    ids_ref, far_in_ref, xb_ref, xa_ref, quads_ref, mask_ref, blob, out_ref,
    wide_zero, wide_one, coarse_ref, up_ref, basis_ref, rim_ref, far_ref, spot_ref, back_ref, down_ref, sem,
):
    first = [
        piece_copy(blob, "up", up_ref, sem.at[0]),
        piece_copy(blob, "basis", basis_ref, sem.at[1]),
        piece_copy(blob, "coarse", coarse_ref, sem.at[2], ids_ref[3], 64),
        piece_copy(blob, "rim", rim_ref, sem.at[3]),
    ]
    tables = [piece_copy(blob, "far", far_ref, sem.at[4 + dx], dx, 2) for dx in range(2)]
    last = [
        piece_copy(blob, "spot", spot_ref, sem.at[6]),
        piece_copy(blob, "back", back_ref, sem.at[7]),
        piece_copy(blob, "down", down_ref, sem.at[8]),
    ]
    for copy in (*first, *tables, *last):
        copy.start()
    three = coarse_rows(quads_ref[...])
    odd = ids_ref[0] == 1
    a, b = xa_ref[...], xb_ref[...]
    low, high = jnp.where(odd, a, b), jnp.where(odd, b, a)
    sides = jnp.concatenate([*split(high), *split(reflected(low))], axis=1)
    for copy in first:
        copy.wait()
    two = up_group(three, up_ref[...])
    mixes = mm(rim_ref[:, :X_ROWS], sides)
    upper = jnp.concatenate([three, two, jnp.zeros((56, 512), F32)], axis=0)
    upper = times_exact(upper, in_columns(basis_ref))
    chosen = jnp.concatenate([coarse_ref[:, :128], coarse_ref[:208, 128:]], axis=0)
    coarse = exact_times(chosen, upper)
    for side in range(2):
        mix = mixes[:, 1024 * side : 1024 * side + 512] + mixes[:, 1024 * side + 512 : 1024 * side + 1024]
        for j in range(9):
            _, ky, kz = KINDS[j]
            place_mix(wide_one, j, ky, kz, mix[RIM * j : RIM * j + RIM], RIM * side)
    for k, (dx, ky, kz) in enumerate(KINDS):
        mix = coarse[SMALL * k : SMALL * k + SMALL]
        if dx == 0:
            place_mix(wide_zero, k % 9, ky, kz, mix, 0)
        elif dx == 1:
            place_mix(wide_one, k % 9, ky, kz, mix, 2 * RIM)
        else:
            place_mix(wide_one, k % 9, ky, kz, reflected(mix), 2 * RIM + SMALL)
    tables[0].wait()
    zero = far_rows(wide_zero, far_ref, 0)
    tables[1].wait()
    one = far_rows(wide_one, far_ref, 1)
    rims = jnp.concatenate([one[:RIM], reflected(one[RIM : 2 * RIM])], axis=0)
    small = zero + one[2 * RIM : 2 * RIM + SMALL] + reflected(one[2 * RIM + SMALL :])
    for copy in last:
        copy.wait()
    far = far_in_ref[...] + exact_times(spot_ref[:, : 2 * RIM], rims)
    far = jnp.concatenate([far[:64], far[64:] + small], axis=0)
    far = times_exact(far, in_columns(back_ref))
    down = whole_down(down_ref)
    local = far[73:74] + downward(only(far[74:75], ids_ref[4]), down)
    local = far[72:73] + downward(only(local[:1], ids_ref[5]), down)
    local = jnp.broadcast_to(local[:1], (8, 512)) * octant_mask(8)
    local = far[64:72] + downward(local, down)
    local = jnp.broadcast_to(local[:, None, :], (8, 8, 512)).reshape(64, 512) * octant_mask(64)
    out_ref[...] = (far[:64] + downward(local, down)) * mask_ref[...]


def pairs(axis, outer):
    result = []
    for i in range(512):
        c = place(i, 3)
        c[axis] = (c[axis] ^ 1) if not outer else c[axis] + (1 if c[axis] % 2 else -1)
        if 0 <= c[axis] < 8:
            result.append((i, morton(*c, 3)))
    return result


def exchange(pa, pb, axis):
    return (
        lax.ppermute(pa, AXES, pairs(axis, False)),
        lax.ppermute(pb, AXES, pairs(axis, True)),
    )


SMEM = pl.BlockSpec(memory_space=pltpu.SMEM)
VMEM = pl.BlockSpec(memory_space=pltpu.VMEM)
HBM = pl.BlockSpec(memory_space=pltpu.HBM)
AXES = ("upper", "bit2", "bit1", "bit0")
LIMIT = 52 * 2**20


def call(kernel, shapes, scratch, ids, vmem_args, hbm_args=(), micros=1):
    return pl.pallas_call(
        kernel,
        out_shape=[jax.ShapeDtypeStruct(shape, F32) for shape in shapes],
        in_specs=[SMEM] + [VMEM] * len(vmem_args) + [HBM] * len(hbm_args),
        out_specs=[VMEM] * len(shapes),
        scratch_shapes=scratch,
        compiler_params=pltpu.CompilerParams(vmem_limit_bytes=LIMIT),
        cost_estimate=pl.CostEstimate(flops=micros * 10**9, bytes_accessed=0, transcendentals=0),
    )(ids, *vmem_args, *hbm_args)


def rows_of(*counts):
    return [(count, 512) for count in counts]


def scratch_rows(*counts):
    return [pltpu.VMEM((count, 512), F32) for count in counts]


def table_scratch(*names):
    return [pltpu.VMEM((PIECES[name], 256), BF16) for name in names]


def wide_scratch(*shape):
    return [pltpu.VMEM(shape, BF16)]


def local(multipoles, occupancy):
    blob = jnp.asarray(constants())
    me = lax.axis_index(AXES)
    parent = me // 8
    ids = jnp.stack([me % 2, me // 2 % 2, me // 4 % 2, parent, parent % 8, me % 8]).astype(jnp.int32)
    own, pa, pb, mask = call(
        upward_kernel,
        rows_of(ROWS, Z_ROWS, Z_ROWS, 64),
        scratch_rows(64)
        + [pltpu.VMEM((1, 512), jnp.int32)]
        + table_scratch("up", "basis")
        + [pltpu.SemaphoreType.DMA((4,))],
        ids, [], [multipoles, occupancy.reshape(1, 512), blob], micros=4,
    )
    za, zb = exchange(pa, pb, 2)
    pa, pb = call(
        y_kernel, rows_of(Y_ROWS, Y_ROWS), scratch_rows(Z_ROWS, Z_ROWS), ids, [own, pa, zb, za]
    )
    ya, yb = exchange(pa, pb, 1)
    ours, theirs = (p[Y_THREE : Y_THREE + 1, :256] for p in (pa, ya))
    quad = jnp.where(jnp.arange(256)[None] // 64 % 2 == ids[1], ours, theirs)
    quads = lax.all_to_all(
        jnp.broadcast_to(quad, (128, 256)), ("upper", "bit0"), 0, 0, tiled=True
    )
    pa, pb = call(
        x_kernel, rows_of(X_ROWS, X_ROWS), scratch_rows(Z_ROWS, Z_ROWS, Y_ROWS, Y_ROWS),
        ids, [own, zb, za, ya, yb], micros=40,
    )
    xa, xb = exchange(pa, pb, 0)
    (far,) = call(
        inner_kernel,
        rows_of(ROWS),
        scratch_rows(256, 128)
        + wide_scratch(4, 2 * ROWS, 9 * 128)
        + wide_scratch(4, 4 * ROWS, 9 * 128)
        + table_scratch("small", "fine", "far")
        + [pltpu.SemaphoreType.DMA((4,))],
        ids, [own, zb, za, ya, yb], [blob], micros=1,
    )
    (out,) = call(
        outer_kernel,
        rows_of(64),
        wide_scratch(4, 2 * SMALL, 9 * 128)
        + wide_scratch(4, 4 * RIM + 4 * SMALL, 9 * 128)
        + wide_scratch(224, 256)
        + table_scratch("up", "basis", "rim", "far", "spot", "back", "down")
        + [pltpu.SemaphoreType.DMA((9,))],
        ids, [far, xb, xa, quads, mask], [blob], micros=4,
    )
    return out


def solution(mesh):
    fine_mesh = Mesh(mesh.devices.reshape(64, 2, 2, 2), AXES)
    return jax.shard_map(
        local,
        mesh=fine_mesh,
        in_specs=(P(AXES, None), P(AXES)),
        out_specs=P(AXES, None),
        check_vma=False,
    )
```

```python
import functools

import jax
import jax.numpy as jnp
import ml_dtypes
import numpy as np
from jax import lax
from jax.experimental import pallas as pl
from jax.experimental.pallas import tpu as pltpu
from jax.sharding import Mesh
from jax.sharding import PartitionSpec as P

F32 = jnp.float32
BF16 = jnp.bfloat16
NODES = np.cos((2.0 * np.arange(4) + 1.0) * (np.pi / 8.0))
ENTRY = np.arange(512)
OCT = [ENTRY // 64 % 2, ENTRY // 128 % 2, ENTRY // 256 % 2]
DEG = [ENTRY // 16 % 4, ENTRY // 4 % 4, ENTRY % 4]
KINDS = [(dx, ky, kz) for dx in (-1, 0, 1) for ky in range(3) for kz in range(3)]
ROWS = 80
SMALL = 16
PIECES = {
    "up": 512, "basis": 1024, "small": 432, "fine": 1728, "rim": 288, "spot": 80, "far": 9216,
    "back": 1024, "down": 512, "coarse": 64 * 224,
}
TABLES = ("up", "basis", "coarse", "rim")


def halves(values):
    high = values.astype(np.float32).astype(ml_dtypes.bfloat16)
    low = (values - high.astype(np.float64)).astype(ml_dtypes.bfloat16)
    return high, low


def table(shift):
    distance = np.zeros((512, 512))
    reach = np.zeros((512, 512), int)
    for d in range(3):
        offset = 2 * shift[d] + OCT[d][:, None] - OCT[d][None, :]
        reach = np.maximum(reach, abs(offset))
        placed = NODES[DEG[d]]
        distance += (offset + 0.5 * (placed[:, None] - placed[None, :])) ** 2
    keep = reach >= 2
    return np.where(keep, 1.0 / np.sqrt(np.where(keep, distance, 1.0)), 0.0)


def upward_matrix():
    def terms(v):
        return [v, 2 * v * v - 1, 4 * v**3 - 3 * v]

    parent = np.arange(64)
    degrees = [parent // 16, parent // 4 % 4, parent % 4]
    result = np.ones((512, 64))
    for d in range(3):
        child = (OCT[d] - 0.5 + 0.5 * NODES[DEG[d]])[:, None]
        place = NODES[degrees[d]][None, :]
        result *= 0.25 + 0.5 * sum(a * b for a, b in zip(terms(place), terms(child)))
    return result


def parity_signs():
    signs = np.zeros((512, 512))
    for q in range(512):
        odd = [q // 64 % 2, q // 128 % 2, q // 256]
        degree = [q // 16 % 4, q // 4 % 4, q % 4]
        for o in range(8):
            octant = [o % 2, o // 2 % 2, o // 4]
            a, b, e = (3 - v if side else v for v, side in zip(degree, octant))
            sign = (-1) ** sum(c * side for c, side in zip(odd, octant))
            signs[64 * o + 16 * a + 4 * b + e, q] = sign
    return signs


def morton(x, y, z, bits):
    return sum(
        (x >> i & 1) << 3 * i | (y >> i & 1) << 3 * i + 1 | (z >> i & 1) << 3 * i + 2
        for i in range(bits)
    )


def place(number, bits):
    return [sum((number >> 3 * i + d & 1) << i for i in range(bits)) for d in range(3)]


Z_ROWS, Y_ROWS, X_ROWS = 24, 40, 64
Z_THREE, Y_THREE = 21, 35
FINE_PARTS = ((0, 64), (0, 16), (0, 16), (0, 24), (0, 24))
SMALL_PARTS = ((64, 80), (16, 24), (16, 24), (24, 40), (24, 40))
RIM = 32


def level_extent(level):
    return 2 ** (level - 4)


def own_row(level, x, y, z):
    return {6: 0, 5: 64, 4: 72}[level] + morton(x, y, z, level - 4)


def z_row(level, x, y):
    n = level_extent(level)
    return {6: 0, 5: 16, 4: 20}[level] + y * n + x


def y_row(level, x, z):
    n = level_extent(level)
    return {6: 0, 5: 24, 4: 32}[level] + (z + 1) * n + x


def x_row(level, y, z):
    n = level_extent(level) + 2
    return {6: 0, 5: 36, 4: 52}[level] + (z + 1) * n + y + 1


def source_row(level, x, y, z):
    n = level_extent(level)
    if not 0 <= y < n:
        part, row = (4 if y >= n else 3), y_row(level, x, z)
    elif not 0 <= z < n:
        part, row = (2 if z >= n else 1), z_row(level, x, y)
    else:
        part, row = 0, own_row(level, x, y, z)
    parts = FINE_PARTS if level == 6 else SMALL_PARTS
    start, stop = parts[part]
    assert start <= row < stop
    return sum(q - p for p, q in parts[:part]) + row - start


def kind_terms(kind):
    return [(0, 1)] if kind == 0 else [(1, 1), (-1, 1 if kind == 1 else -1)]


def rim_target(level, y, z):
    return {6: 0, 5: 16, 4: 20}[level] + z * level_extent(level) + y


def selections():
    fine = np.zeros((27, 64, 256))
    small = np.zeros((27, SMALL, 128))
    rim = np.zeros((9, RIM, 256))
    spot = np.zeros((ROWS, 256))
    for k, (dx, ky, kz) in enumerate(KINDS):
        for dy, sy in kind_terms(ky):
            for dz, sz in kind_terms(kz):
                for level in (6, 5, 4):
                    n = level_extent(level)
                    factor = sy * sz * 2.0 ** (level - 6)
                    into = fine[k] if level == 6 else small[k]
                    for m in range(n**3):
                        x, y, z = place(m, level - 4)
                        row = own_row(level, x, y, z) % 64
                        if 0 <= x + dx < n:
                            into[row, source_row(level, x + dx, y + dy, z + dz)] += factor
                        elif dx == 1:
                            rim[k - 18, rim_target(level, y, z), x_row(level, y + dy, z + dz)] += factor
                            spot[own_row(level, x, y, z), rim_target(level, y, z)] = 1
                        else:
                            spot[own_row(level, x, y, z), RIM + rim_target(level, y, z)] = 1
    coarse = np.zeros((64, 27, SMALL, 128))
    for parent in range(64):
        for level, row, base in ((3, 9, 0), (2, 10, 64)):
            bits = level - 1
            n = 2**bits
            x, y, z = place(parent >> 3 * (2 - bits), bits)
            for k, (dx, ky, kz) in enumerate(KINDS):
                for dy, sy in kind_terms(ky):
                    for dz, sz in kind_terms(kz):
                        u = (x + dx, y + dy, z + dz)
                        if all(0 <= c < n for c in u):
                            coarse[parent, k, row, base + morton(*u, bits)] += (
                                sy * sz * 2.0 ** (level - 6)
                            )
    coarse = np.pad(coarse.reshape(64, 27 * SMALL, 128), ((0, 0), (0, 16), (0, 0)))
    return {
        "small": np.pad(small.reshape(27 * SMALL, 128), ((0, 0), (0, 128))),
        "fine": fine.reshape(27 * 64, 256),
        "rim": rim.reshape(9 * RIM, 256),
        "spot": spot,
        "coarse": np.concatenate(np.split(coarse, 2, axis=1), axis=2).reshape(64 * 224, 256),
    }


@functools.lru_cache(maxsize=1)
def constants():
    basis, back = 0.5 * parity_signs(), 0.25 * parity_signs().T
    tables = {
        (dx, dy, dz): back @ table((dx, dy, dz)) @ basis
        for dx in (0, 1)
        for dy in (0, 1)
        for dz in (0, 1)
    }
    far = np.zeros((2, 4, 9 * 128, 256), ml_dtypes.bfloat16)
    for t in range(4):
        for k, (dx, ky, kz) in enumerate(KINDS[9:]):
            c = source_class(t, ky, kz)
            block = tables[dx, min(ky, 1), min(kz, 1)][
                128 * c : 128 * c + 128, 128 * t : 128 * t + 128
            ]
            high, low = halves(block)
            j = 128 * (k % 9)
            far[dx, t, j : j + 128, :128] = high
            far[dx, t, j : j + 128, 128:] = low
    up = upward_matrix()
    wide_down = np.concatenate(halves(np.tile(up.T, (2, 1))), axis=1)
    pieces = selections() | {
        "up": np.concatenate(halves(np.tile(up, (1, 2))), axis=1),
        "basis": in_lanes(basis),
        "far": far.reshape(-1, 256),
        "back": in_lanes(back),
        "down": in_lanes(wide_down),
    }
    assert {name: len(piece) for name, piece in pieces.items()} == PIECES
    return np.concatenate([pieces[name].astype(ml_dtypes.bfloat16) for name in PIECES])


def in_lanes(matrix):
    return np.concatenate(np.split(matrix, matrix.shape[1] // 256, axis=1))


def source_class(t, ky, kz):
    return t ^ ((ky == 2) | (kz == 2) << 1)


def split(values):
    high = values.astype(BF16)
    return high, (values - high.astype(F32)).astype(BF16)


def mm(a, b):
    return jnp.dot(a, b, preferred_element_type=F32)


def stacked(values):
    rows, width = values.shape
    if rows % 16:
        values = jnp.concatenate([values, jnp.zeros((16 - rows % 16, width), F32)], axis=0)
    return jnp.concatenate(split(values), axis=0)


def times_exact(values, matrix):
    product = mm(stacked(values), matrix)
    half = product.shape[0] // 2
    return (product[:half] + product[half:])[: values.shape[0]]


def times_pair(values, matrix):
    product = mm(stacked(values), matrix)
    half = product.shape[0] // 2
    width = product.shape[1] // 2
    total = product[:half, :width] + product[half:, :width] + product[:half, width:]
    return total[: values.shape[0]]


def exact_times(matrix, values):
    product = mm(matrix, jnp.concatenate(split(values), axis=1))
    width = values.shape[1]
    return product[:, :width] + product[:, width:]


def piece_copy(blob, name, ref, sem, part=0, parts=1):
    start = sum(list(PIECES.values())[: list(PIECES).index(name)])
    rows = PIECES[name] // parts
    source = blob.at[pl.ds(pl.multiple_of(start + part * rows, 16), rows)]
    target = ref if ref.shape[0] == rows else ref.at[pl.ds(part * rows, rows)]
    return pltpu.make_async_copy(source, target, sem)


def in_columns(ref):
    rows = ref.shape[0] // 2
    return jnp.concatenate([ref[:rows], ref[rows:]], axis=1)


def iota(shape, axis):
    return lax.broadcasted_iota(jnp.int32, shape, axis)


def octant_mask(rows):
    return (iota((rows, 512), 1) // 64 == iota((rows, 512), 0) % 8).astype(F32)


def occupancy_mask(occ):
    kept = jnp.where(
        iota((64, 512), 1) // 8 == iota((64, 512), 0), jnp.broadcast_to(occ.astype(F32), (64, 512)), 0.0
    )
    spread = iota((512, 512), 0) % 8 == iota((512, 512), 1) // 64
    return mm(kept.astype(BF16), jnp.where(spread, 1.0, 0.0).astype(BF16))


def upward(values, up):
    twice = times_pair(values, up)
    return jnp.concatenate([twice] * 4, axis=1)


def up_group(values, up):
    rows = values.shape[0]
    return (upward(values, up) * octant_mask(rows)).reshape(rows // 8, 8, 512).sum(axis=1)


def downward(masked, down):
    folded = masked[:, :128] + masked[:, 128:256] + masked[:, 256:384] + masked[:, 384:]
    return times_pair(folded, down)


def upward_kernel(
    ids_ref, mult_ref, occ_ref, blob, own_ref, pa_ref, pb_ref, mask_ref, up_ref, basis_ref, sem
):
    up_copy = piece_copy(blob, "up", up_ref, sem.at[0])
    basis_copy = piece_copy(blob, "basis", basis_ref, sem.at[1])
    up_copy.start()
    basis_copy.start()
    mask_ref[...] = occupancy_mask(occ_ref[...])
    up_copy.wait()
    grouped_six = mult_ref[...] * mask_ref[...]
    grouped_five = up_group(grouped_six, up_ref[...])
    grouped_four = up_group(grouped_five, up_ref[...])
    three = upward(jnp.broadcast_to(grouped_four, (8, 512)), up_ref[...])
    basis_copy.wait()
    basis = in_columns(basis_ref)
    own_ref[0:64] = times_exact(grouped_six, basis)
    rest = jnp.concatenate([grouped_five, jnp.broadcast_to(grouped_four, (8, 512))], axis=0)
    own_ref[64:80] = times_exact(rest, basis)
    odd = ids_ref[2] == 1
    for p_ref in (pa_ref, pb_ref):
        p_ref[Z_ROWS - 8 :] = three
    for level in (6, 5, 4):
        n = level_extent(level)
        for y in range(n):
            for x in range(n):
                low = own_ref[pl.ds(own_row(level, x, y, 0), 1)]
                high = own_ref[pl.ds(own_row(level, x, y, n - 1), 1)]
                i = z_row(level, x, y)
                pa_ref[pl.ds(i, 1)] = jnp.where(odd, low, high)
                pb_ref[pl.ds(i, 1)] = jnp.where(odd, high, low)


def sort_sides(odd, ra_ref, rb_ref, low_ref, high_ref):
    a, b = ra_ref[...], rb_ref[...]
    low_ref[...] = jnp.where(odd, a, b)
    high_ref[...] = jnp.where(odd, b, a)


def y_kernel(ids_ref, own_ref, sent_ref, zb_ref, za_ref, pa_ref, pb_ref, zl, zh):
    sort_sides(ids_ref[2] == 1, za_ref, zb_ref, zl, zh)
    odd = ids_ref[1] == 1
    pa_ref[...] = jnp.zeros_like(pa_ref)
    pb_ref[...] = jnp.zeros_like(pb_ref)
    mine, other = sent_ref[pl.ds(Z_THREE, 1)], za_ref[pl.ds(Z_THREE, 1)]
    pa_ref[pl.ds(Y_THREE, 1)] = jnp.where(
        iota((1, 512), 1) // 128 % 2 == ids_ref[2], mine, other
    )

    def get(level, x, y, z):
        n = level_extent(level)
        if z < 0:
            return zl[pl.ds(z_row(level, x, y), 1)]
        if z >= n:
            return zh[pl.ds(z_row(level, x, y), 1)]
        return own_ref[pl.ds(own_row(level, x, y, z), 1)]

    for level in (6, 5, 4):
        n = level_extent(level)
        for z in range(-1, n + 1):
            for x in range(n):
                low, high = get(level, x, 0, z), get(level, x, n - 1, z)
                i = y_row(level, x, z)
                pa_ref[pl.ds(i, 1)] = jnp.where(odd, low, high)
                pb_ref[pl.ds(i, 1)] = jnp.where(odd, high, low)


def x_kernel(ids_ref, own_ref, zb_ref, za_ref, ya_ref, yb_ref, pa_ref, pb_ref, zl, zh, yl, yh):
    sort_sides(ids_ref[2] == 1, za_ref, zb_ref, zl, zh)
    sort_sides(ids_ref[1] == 1, ya_ref, yb_ref, yl, yh)
    odd = ids_ref[0] == 1
    pa_ref[...] = jnp.zeros_like(pa_ref)
    pb_ref[...] = jnp.zeros_like(pb_ref)

    def get(level, x, y, z):
        n = level_extent(level)
        if y < 0:
            return yl[pl.ds(y_row(level, x, z), 1)]
        if y >= n:
            return yh[pl.ds(y_row(level, x, z), 1)]
        if z < 0:
            return zl[pl.ds(z_row(level, x, y), 1)]
        if z >= n:
            return zh[pl.ds(z_row(level, x, y), 1)]
        return own_ref[pl.ds(own_row(level, x, y, z), 1)]

    for level in (6, 5, 4):
        n = level_extent(level)
        for z in range(-1, n + 1):
            for y in range(-1, n + 1):
                low, high = get(level, 0, y, z), get(level, n - 1, y, z)
                i = x_row(level, y, z)
                pa_ref[pl.ds(i, 1)] = jnp.where(odd, low, high)
                pb_ref[pl.ds(i, 1)] = jnp.where(odd, high, low)


def coarse_rows(quads):
    half = iota((128, 128), 1) // 64
    keep = half == iota((128, 128), 0) % 2
    blocks = []
    for i in range(4):
        pair = quads[:, 128 * (i // 2) : 128 * (i // 2) + 128]
        both = jnp.where(half == i % 2, pair, pltpu.roll(pair, 64, 1))
        blocks.append(jnp.where(keep, both, 0.0))
    gather = jnp.where(iota((64, 128), 0) == iota((64, 128), 1) // 2, 1.0, 0.0).astype(BF16)
    return exact_times(gather, jnp.concatenate(blocks, axis=1))


def place_mix(wide, j, ky, kz, mix, row):
    rows, half = mix.shape[0], wide.shape[1] // 2
    high, low = split(mix)
    for t in range(4):
        c = source_class(t, ky, kz)
        wide[t, row : row + rows, 128 * j : 128 * j + 128] = high[:, 128 * c : 128 * c + 128]
        wide[t, half + row : half + row + rows, 128 * j : 128 * j + 128] = low[:, 128 * c : 128 * c + 128]


def far_rows(wide, far_ref, dx):
    parts = []
    for t in range(4):
        rows = 1152 * (4 * dx + t)
        product = mm(wide[t], far_ref[rows : rows + 1152])
        half = product.shape[0] // 2
        top, bottom = product[:half], product[half:]
        parts.append((top[:, :128] + bottom[:, :128]) + (top[:, 128:] + bottom[:, 128:]))
    return jnp.concatenate(parts, axis=1)


def reflected(rows):
    return jnp.where(iota(rows.shape, 1) // 64 % 2 == 1, -rows, rows)


def whole_down(down_ref):
    return jnp.concatenate([down_ref[128 * i : 128 * i + 128] for i in range(4)], axis=1)


def only(row, octant):
    kept = iota((8, 512), 1) // 64 == octant
    return jnp.where(kept, jnp.broadcast_to(row, (8, 512)), 0.0)


def inner_kernel(
    ids_ref, own_ref, zb_ref, za_ref, ya_ref, yb_ref, blob, out_ref, up_ref, basis_ref, coarse_ref, rim_ref,
    fine_src, small_src, wide_zero, wide_one, small_ref, fine_ref, far_ref, sem,
):
    later = [
        piece_copy(blob, "up", up_ref, sem.at[4]),
        piece_copy(blob, "basis", basis_ref, sem.at[5]),
        piece_copy(blob, "coarse", coarse_ref, sem.at[6], ids_ref[3], 64),
        piece_copy(blob, "rim", rim_ref, sem.at[7]),
    ]
    small_copy = piece_copy(blob, "small", small_ref, sem.at[0])
    fine_copy = piece_copy(blob, "fine", fine_ref, sem.at[1])
    tables = [piece_copy(blob, "far", far_ref, sem.at[2 + dx], dx, 2) for dx in range(2)]
    for copy in (small_copy, fine_copy, *tables, *later):
        copy.start()
    fine_src[144:] = jnp.zeros((112, 512), F32)
    small_src[64:] = jnp.zeros((64, 512), F32)
    stack = [own_ref[...]]
    for axis, ra_ref, rb_ref in ((2, za_ref, zb_ref), (1, ya_ref, yb_ref)):
        odd = ids_ref[axis] == 1
        a, b = ra_ref[...], rb_ref[...]
        stack += [jnp.where(odd, a, b), jnp.where(odd, b, a)]
    for target, parts in ((fine_src, FINE_PARTS), (small_src, SMALL_PARTS)):
        base = 0
        for values, (start, stop) in zip(stack, parts):
            target[base : base + stop - start] = values[start:stop]
            base += stop - start
    small_copy.wait()
    small = exact_times(small_ref[:, :128], small_src[...])
    fine_split = jnp.concatenate(split(fine_src[...]), axis=1)
    fine_copy.wait()
    far = 0.0
    for group in (1, 0, 2):
        mixes = mm(fine_ref[576 * group : 576 * group + 576], fine_split)
        mixes = mixes[:, :512] + mixes[:, 512:]
        for j in range(9):
            k = 9 * group + j
            _, ky, kz = KINDS[k]
            mix = [mixes[64 * j : 64 * j + 64], small[SMALL * k : SMALL * k + SMALL]]
            mix = jnp.concatenate(mix, axis=0)
            if group == 1:
                place_mix(wide_zero, j, ky, kz, mix, 0)
            else:
                mix = reflected(mix) if group == 0 else mix
                place_mix(wide_one, j, ky, kz, mix, ROWS if group == 0 else 0)
        if group == 1:
            tables[0].wait()
            far = far_rows(wide_zero, far_ref, 0)
    tables[1].wait()
    both = far_rows(wide_one, far_ref, 1)
    out_ref[...] = far + both[:ROWS] + reflected(both[ROWS:])
    for copy in later:
        copy.wait()


def outer_kernel(
    ids_ref, far_in_ref, xa_ref, xb_ref, quads_ref, mask_ref, up_ref, basis_ref, coarse_ref, rim_ref, blob, out_ref,
    wide_zero, wide_one, far_ref, spot_ref, back_ref, down_ref, sem,
):
    tables = [piece_copy(blob, "far", far_ref, sem.at[dx], dx, 2) for dx in range(2)]
    last = [
        piece_copy(blob, "spot", spot_ref, sem.at[2]),
        piece_copy(blob, "back", back_ref, sem.at[3]),
        piece_copy(blob, "down", down_ref, sem.at[4]),
    ]
    for copy in (*tables, *last):
        copy.start()
    three = coarse_rows(quads_ref[...])
    odd = ids_ref[0] == 1
    a, b = xa_ref[...], xb_ref[...]
    low, high = jnp.where(odd, a, b), jnp.where(odd, b, a)
    sides = jnp.concatenate([*split(high), *split(reflected(low))], axis=1)
    two = up_group(three, up_ref[...])
    mixes = mm(rim_ref[:, :X_ROWS], sides)
    upper = jnp.concatenate([three, two, jnp.zeros((56, 512), F32)], axis=0)
    upper = times_exact(upper, in_columns(basis_ref))
    chosen = jnp.concatenate([coarse_ref[:, :128], coarse_ref[:208, 128:]], axis=0)
    coarse = exact_times(chosen, upper)
    for side in range(2):
        mix = mixes[:, 1024 * side : 1024 * side + 512] + mixes[:, 1024 * side + 512 : 1024 * side + 1024]
        for j in range(9):
            _, ky, kz = KINDS[j]
            place_mix(wide_one, j, ky, kz, mix[RIM * j : RIM * j + RIM], RIM * side)
    for k, (dx, ky, kz) in enumerate(KINDS):
        mix = coarse[SMALL * k : SMALL * k + SMALL]
        if dx == 0:
            place_mix(wide_zero, k % 9, ky, kz, mix, 0)
        elif dx == 1:
            place_mix(wide_one, k % 9, ky, kz, mix, 2 * RIM)
        else:
            place_mix(wide_one, k % 9, ky, kz, reflected(mix), 2 * RIM + SMALL)
    tables[0].wait()
    zero = far_rows(wide_zero, far_ref, 0)
    tables[1].wait()
    one = far_rows(wide_one, far_ref, 1)
    rims = jnp.concatenate([one[:RIM], reflected(one[RIM : 2 * RIM])], axis=0)
    small = zero + one[2 * RIM : 2 * RIM + SMALL] + reflected(one[2 * RIM + SMALL :])
    for copy in last:
        copy.wait()
    far = far_in_ref[...] + exact_times(spot_ref[:, : 2 * RIM], rims)
    far = jnp.concatenate([far[:64], far[64:] + small], axis=0)
    far = times_exact(far, in_columns(back_ref))
    down = whole_down(down_ref)
    local = far[73:74] + downward(only(far[74:75], ids_ref[4]), down)
    local = far[72:73] + downward(only(local[:1], ids_ref[5]), down)
    local = jnp.broadcast_to(local[:1], (8, 512)) * octant_mask(8)
    local = far[64:72] + downward(local, down)
    local = jnp.broadcast_to(local[:, None, :], (8, 8, 512)).reshape(64, 512) * octant_mask(64)
    out_ref[...] = (far[:64] + downward(local, down)) * mask_ref[...]


def pairs(axis, outer):
    result = []
    for i in range(512):
        c = place(i, 3)
        c[axis] = (c[axis] ^ 1) if not outer else c[axis] + (1 if c[axis] % 2 else -1)
        if 0 <= c[axis] < 8:
            result.append((i, morton(*c, 3)))
    return result


def exchange(pa, pb, axis):
    return (
        lax.ppermute(pa, AXES, pairs(axis, False)),
        lax.ppermute(pb, AXES, pairs(axis, True)),
    )


SMEM = pl.BlockSpec(memory_space=pltpu.SMEM)
VMEM = pl.BlockSpec(memory_space=pltpu.VMEM)
HBM = pl.BlockSpec(memory_space=pltpu.HBM)
AXES = ("upper", "bit2", "bit1", "bit0")
LIMIT = 52 * 2**20


def call(kernel, shapes, scratch, ids, vmem_args, hbm_args=(), micros=1):
    return pl.pallas_call(
        kernel,
        out_shape=[jax.ShapeDtypeStruct(shape[:2], (*shape, F32)[2]) for shape in shapes],
        in_specs=[SMEM] + [VMEM] * len(vmem_args) + [HBM] * len(hbm_args),
        out_specs=[VMEM] * len(shapes),
        scratch_shapes=scratch,
        compiler_params=pltpu.CompilerParams(vmem_limit_bytes=LIMIT),
        cost_estimate=pl.CostEstimate(flops=micros * 10**9, bytes_accessed=0, transcendentals=0),
    )(ids, *vmem_args, *hbm_args)


def rows_of(*counts):
    return [(count, 512) for count in counts]


def scratch_rows(*counts):
    return [pltpu.VMEM((count, 512), F32) for count in counts]


def table_scratch(*names):
    return [pltpu.VMEM((PIECES[name], 256), BF16) for name in names]


def wide_scratch(*shape):
    return [pltpu.VMEM(shape, BF16)]


def local(multipoles, occupancy):
    blob = jnp.asarray(constants())
    me = lax.axis_index(AXES)
    parent = me // 8
    ids = jnp.stack([me % 2, me // 2 % 2, me // 4 % 2, parent, parent % 8, me % 8]).astype(jnp.int32)
    own, pa, pb, mask = call(
        upward_kernel,
        rows_of(ROWS, Z_ROWS, Z_ROWS, 64),
        table_scratch("up", "basis") + [pltpu.SemaphoreType.DMA((2,))],
        ids, [multipoles, occupancy.reshape(1, 512)], [blob], micros=4,
    )
    za, zb = exchange(pa, pb, 2)
    pa, pb = call(
        y_kernel, rows_of(Y_ROWS, Y_ROWS), scratch_rows(Z_ROWS, Z_ROWS), ids, [own, pa, zb, za]
    )
    ya, yb = exchange(pa, pb, 1)
    ours, theirs = (p[Y_THREE : Y_THREE + 1, :256] for p in (pa, ya))
    quad = jnp.where(jnp.arange(256)[None] // 64 % 2 == ids[1], ours, theirs)
    quads = lax.all_to_all(
        jnp.broadcast_to(quad, (128, 256)), ("upper", "bit0"), 0, 0, tiled=True
    )
    pa, pb = call(
        x_kernel, rows_of(X_ROWS, X_ROWS), scratch_rows(Z_ROWS, Z_ROWS, Y_ROWS, Y_ROWS),
        ids, [own, zb, za, ya, yb], micros=40,
    )
    xa, xb = exchange(pa, pb, 0)
    far, *tables = call(
        inner_kernel,
        rows_of(ROWS) + [(PIECES[n] // (64 if n == "coarse" else 1), 256, BF16) for n in TABLES],
        scratch_rows(256, 128)
        + wide_scratch(4, 2 * ROWS, 9 * 128)
        + wide_scratch(4, 4 * ROWS, 9 * 128)
        + table_scratch("small", "fine", "far")
        + [pltpu.SemaphoreType.DMA((8,))],
        ids, [own, zb, za, ya, yb], [blob], micros=1,
    )
    (out,) = call(
        outer_kernel,
        rows_of(64),
        wide_scratch(4, 2 * SMALL, 9 * 128)
        + wide_scratch(4, 4 * RIM + 4 * SMALL, 9 * 128)
        + table_scratch("far", "spot", "back", "down")
        + [pltpu.SemaphoreType.DMA((5,))],
        ids, [far, xa, xb, quads, mask, *tables], [blob], micros=4,
    )
    return out


def solution(mesh):
    fine_mesh = Mesh(mesh.devices.reshape(64, 2, 2, 2), AXES)
    return jax.shard_map(
        local,
        mesh=fine_mesh,
        in_specs=(P(AXES, None), P(AXES)),
        out_specs=P(AXES, None),
        check_vma=False,
    )
```

```python
import functools

import jax
import jax.numpy as jnp
import ml_dtypes
import numpy as np
from jax import lax
from jax.experimental import pallas as pl
from jax.experimental.pallas import tpu as pltpu
from jax.sharding import Mesh
from jax.sharding import PartitionSpec as P

F32 = jnp.float32
BF16 = jnp.bfloat16
NODES = np.cos((2.0 * np.arange(4) + 1.0) * (np.pi / 8.0))
ENTRY = np.arange(512)
OCT = [ENTRY // 64 % 2, ENTRY // 128 % 2, ENTRY // 256 % 2]
DEG = [ENTRY // 16 % 4, ENTRY // 4 % 4, ENTRY % 4]
KINDS = [(dx, ky, kz) for dx in (-1, 0, 1) for ky in range(3) for kz in range(3)]
ROWS = 80
SMALL = 16
PIECES = {
    "up": 512, "basis": 1024, "small": 432, "fine": 1728, "rim": 288, "spot": 80, "far": 9216,
    "back": 1024, "down": 512, "coarse": 64 * 224,
}
TABLES = ("up", "basis", "coarse", "rim")


def halves(values):
    high = values.astype(np.float32).astype(ml_dtypes.bfloat16)
    low = (values - high.astype(np.float64)).astype(ml_dtypes.bfloat16)
    return high, low


def table(shift):
    distance = np.zeros((512, 512))
    reach = np.zeros((512, 512), int)
    for d in range(3):
        offset = 2 * shift[d] + OCT[d][:, None] - OCT[d][None, :]
        reach = np.maximum(reach, abs(offset))
        placed = NODES[DEG[d]]
        distance += (offset + 0.5 * (placed[:, None] - placed[None, :])) ** 2
    keep = reach >= 2
    return np.where(keep, 1.0 / np.sqrt(np.where(keep, distance, 1.0)), 0.0)


def upward_matrix():
    def terms(v):
        return [v, 2 * v * v - 1, 4 * v**3 - 3 * v]

    parent = np.arange(64)
    degrees = [parent // 16, parent // 4 % 4, parent % 4]
    result = np.ones((512, 64))
    for d in range(3):
        child = (OCT[d] - 0.5 + 0.5 * NODES[DEG[d]])[:, None]
        place = NODES[degrees[d]][None, :]
        result *= 0.25 + 0.5 * sum(a * b for a, b in zip(terms(place), terms(child)))
    return result


def parity_signs():
    signs = np.zeros((512, 512))
    for q in range(512):
        odd = [q // 64 % 2, q // 128 % 2, q // 256]
        degree = [q // 16 % 4, q // 4 % 4, q % 4]
        for o in range(8):
            octant = [o % 2, o // 2 % 2, o // 4]
            a, b, e = (3 - v if side else v for v, side in zip(degree, octant))
            sign = (-1) ** sum(c * side for c, side in zip(odd, octant))
            signs[64 * o + 16 * a + 4 * b + e, q] = sign
    return signs


def morton(x, y, z, bits):
    return sum(
        (x >> i & 1) << 3 * i | (y >> i & 1) << 3 * i + 1 | (z >> i & 1) << 3 * i + 2
        for i in range(bits)
    )


def place(number, bits):
    return [sum((number >> 3 * i + d & 1) << i for i in range(bits)) for d in range(3)]


Z_ROWS, Y_ROWS, X_ROWS = 24, 40, 64
Z_THREE, Y_THREE = 21, 35
FINE_PARTS = ((0, 64), (0, 16), (0, 16), (0, 24), (0, 24))
SMALL_PARTS = ((64, 80), (16, 24), (16, 24), (24, 40), (24, 40))
RIM = 32


def level_extent(level):
    return 2 ** (level - 4)


def own_row(level, x, y, z):
    return {6: 0, 5: 64, 4: 72}[level] + morton(x, y, z, level - 4)


def z_row(level, x, y):
    n = level_extent(level)
    return {6: 0, 5: 16, 4: 20}[level] + y * n + x


def y_row(level, x, z):
    n = level_extent(level)
    return {6: 0, 5: 24, 4: 32}[level] + (z + 1) * n + x


def x_row(level, y, z):
    n = level_extent(level) + 2
    return {6: 0, 5: 36, 4: 52}[level] + (z + 1) * n + y + 1


def source_row(level, x, y, z):
    n = level_extent(level)
    if not 0 <= y < n:
        part, row = (4 if y >= n else 3), y_row(level, x, z)
    elif not 0 <= z < n:
        part, row = (2 if z >= n else 1), z_row(level, x, y)
    else:
        part, row = 0, own_row(level, x, y, z)
    parts = FINE_PARTS if level == 6 else SMALL_PARTS
    start, stop = parts[part]
    assert start <= row < stop
    return sum(q - p for p, q in parts[:part]) + row - start


def kind_terms(kind):
    return [(0, 1)] if kind == 0 else [(1, 1), (-1, 1 if kind == 1 else -1)]


def rim_target(level, y, z):
    return {6: 0, 5: 16, 4: 20}[level] + z * level_extent(level) + y


def selections():
    fine = np.zeros((27, 64, 256))
    small = np.zeros((27, SMALL, 128))
    rim = np.zeros((9, RIM, 256))
    spot = np.zeros((ROWS, 256))
    for k, (dx, ky, kz) in enumerate(KINDS):
        for dy, sy in kind_terms(ky):
            for dz, sz in kind_terms(kz):
                for level in (6, 5, 4):
                    n = level_extent(level)
                    factor = sy * sz * 2.0 ** (level - 6)
                    into = fine[k] if level == 6 else small[k]
                    for m in range(n**3):
                        x, y, z = place(m, level - 4)
                        row = own_row(level, x, y, z) % 64
                        if 0 <= x + dx < n:
                            into[row, source_row(level, x + dx, y + dy, z + dz)] += factor
                        elif dx == 1:
                            rim[k - 18, rim_target(level, y, z), x_row(level, y + dy, z + dz)] += factor
                            spot[own_row(level, x, y, z), rim_target(level, y, z)] = 1
                        else:
                            spot[own_row(level, x, y, z), RIM + rim_target(level, y, z)] = 1
    coarse = np.zeros((64, 27, SMALL, 128))
    for parent in range(64):
        for level, row, base in ((3, 9, 0), (2, 10, 64)):
            bits = level - 1
            n = 2**bits
            x, y, z = place(parent >> 3 * (2 - bits), bits)
            for k, (dx, ky, kz) in enumerate(KINDS):
                for dy, sy in kind_terms(ky):
                    for dz, sz in kind_terms(kz):
                        u = (x + dx, y + dy, z + dz)
                        if all(0 <= c < n for c in u):
                            coarse[parent, k, row, base + morton(*u, bits)] += (
                                sy * sz * 2.0 ** (level - 6)
                            )
    coarse = np.pad(coarse.reshape(64, 27 * SMALL, 128), ((0, 0), (0, 16), (0, 0)))
    return {
        "small": np.pad(small.reshape(27 * SMALL, 128), ((0, 0), (0, 128))),
        "fine": fine.reshape(27 * 64, 256),
        "rim": rim.reshape(9 * RIM, 256),
        "spot": spot,
        "coarse": np.concatenate(np.split(coarse, 2, axis=1), axis=2).reshape(64 * 224, 256),
    }


@functools.lru_cache(maxsize=1)
def constants():
    basis, back = 0.5 * parity_signs(), 0.25 * parity_signs().T
    tables = {
        (dx, dy, dz): back @ table((dx, dy, dz)) @ basis
        for dx in (0, 1)
        for dy in (0, 1)
        for dz in (0, 1)
    }
    far = np.zeros((2, 4, 9 * 128, 256), ml_dtypes.bfloat16)
    for t in range(4):
        for k, (dx, ky, kz) in enumerate(KINDS[9:]):
            c = source_class(t, ky, kz)
            block = tables[dx, min(ky, 1), min(kz, 1)][
                128 * c : 128 * c + 128, 128 * t : 128 * t + 128
            ]
            high, low = halves(block)
            j = 128 * (k % 9)
            far[dx, t, j : j + 128, :128] = high
            far[dx, t, j : j + 128, 128:] = low
    up = upward_matrix()
    wide_down = np.concatenate(halves(np.tile(up.T, (2, 1))), axis=1)
    pieces = selections() | {
        "up": np.concatenate(halves(np.tile(up, (1, 2))), axis=1),
        "basis": in_lanes(basis),
        "far": far.reshape(-1, 256),
        "back": in_lanes(back),
        "down": in_lanes(wide_down),
    }
    assert {name: len(piece) for name, piece in pieces.items()} == PIECES
    return np.concatenate([pieces[name].astype(ml_dtypes.bfloat16) for name in PIECES])


def in_lanes(matrix):
    return np.concatenate(np.split(matrix, matrix.shape[1] // 256, axis=1))


def source_class(t, ky, kz):
    return t ^ ((ky == 2) | (kz == 2) << 1)


def split(values):
    high = values.astype(BF16)
    return high, (values - high.astype(F32)).astype(BF16)


def mm(a, b):
    return jnp.dot(a, b, preferred_element_type=F32)


def stacked(values):
    rows, width = values.shape
    if rows % 16:
        values = jnp.concatenate([values, jnp.zeros((16 - rows % 16, width), F32)], axis=0)
    return jnp.concatenate(split(values), axis=0)


def times_exact(values, matrix):
    product = mm(stacked(values), matrix)
    half = product.shape[0] // 2
    return (product[:half] + product[half:])[: values.shape[0]]


def times_pair(values, matrix):
    product = mm(stacked(values), matrix)
    half = product.shape[0] // 2
    width = product.shape[1] // 2
    total = product[:half, :width] + product[half:, :width] + product[:half, width:]
    return total[: values.shape[0]]


def exact_times(matrix, values):
    product = mm(matrix, jnp.concatenate(split(values), axis=1))
    width = values.shape[1]
    return product[:, :width] + product[:, width:]


def piece_copy(blob, name, ref, sem, part=0, parts=1):
    start = sum(list(PIECES.values())[: list(PIECES).index(name)])
    rows = PIECES[name] // parts
    source = blob.at[pl.ds(pl.multiple_of(start + part * rows, 16), rows)]
    target = ref if ref.shape[0] == rows else ref.at[pl.ds(part * rows, rows)]
    return pltpu.make_async_copy(source, target, sem)


def in_columns(ref):
    rows = ref.shape[0] // 2
    return jnp.concatenate([ref[:rows], ref[rows:]], axis=1)


def iota(shape, axis):
    return lax.broadcasted_iota(jnp.int32, shape, axis)


def octant_mask(rows):
    return (iota((rows, 512), 1) // 64 == iota((rows, 512), 0) % 8).astype(F32)


def occupancy_mask(occ):
    kept = jnp.where(
        iota((64, 512), 1) // 8 == iota((64, 512), 0), jnp.broadcast_to(occ.astype(F32), (64, 512)), 0.0
    )
    spread = iota((512, 512), 0) % 8 == iota((512, 512), 1) // 64
    return mm(kept.astype(BF16), jnp.where(spread, 1.0, 0.0).astype(BF16))


def upward(values, up):
    twice = times_pair(values, up)
    return jnp.concatenate([twice] * 4, axis=1)


def up_group(values, up):
    rows = values.shape[0]
    return (upward(values, up) * octant_mask(rows)).reshape(rows // 8, 8, 512).sum(axis=1)


def downward(masked, down):
    folded = masked[:, :128] + masked[:, 128:256] + masked[:, 256:384] + masked[:, 384:]
    return times_pair(folded, down)


def upward_kernel(
    ids_ref, mult_ref, occ_ref, blob, own_ref, pa_ref, pb_ref, mask_ref, up_ref, basis_ref, sem
):
    up_copy = piece_copy(blob, "up", up_ref, sem.at[0])
    basis_copy = piece_copy(blob, "basis", basis_ref, sem.at[1])
    up_copy.start()
    basis_copy.start()
    mask_ref[...] = occupancy_mask(occ_ref[...])
    up_copy.wait()
    grouped_six = mult_ref[...] * mask_ref[...]
    grouped_five = up_group(grouped_six, up_ref[...])
    grouped_four = up_group(grouped_five, up_ref[...])
    three = upward(jnp.broadcast_to(grouped_four, (8, 512)), up_ref[...])
    basis_copy.wait()
    basis = in_columns(basis_ref)
    own_ref[0:64] = times_exact(grouped_six, basis)
    rest = jnp.concatenate([grouped_five, jnp.broadcast_to(grouped_four, (8, 512))], axis=0)
    own_ref[64:80] = times_exact(rest, basis)
    odd = ids_ref[2] == 1
    for p_ref in (pa_ref, pb_ref):
        p_ref[Z_ROWS - 8 :] = three
    for level in (6, 5, 4):
        n = level_extent(level)
        for y in range(n):
            for x in range(n):
                low = own_ref[pl.ds(own_row(level, x, y, 0), 1)]
                high = own_ref[pl.ds(own_row(level, x, y, n - 1), 1)]
                i = z_row(level, x, y)
                pa_ref[pl.ds(i, 1)] = jnp.where(odd, low, high)
                pb_ref[pl.ds(i, 1)] = jnp.where(odd, high, low)


def sort_sides(odd, ra_ref, rb_ref, low_ref, high_ref):
    a, b = ra_ref[...], rb_ref[...]
    low_ref[...] = jnp.where(odd, a, b)
    high_ref[...] = jnp.where(odd, b, a)


def y_kernel(ids_ref, own_ref, sent_ref, zb_ref, za_ref, pa_ref, pb_ref, zl, zh):
    sort_sides(ids_ref[2] == 1, za_ref, zb_ref, zl, zh)
    odd = ids_ref[1] == 1
    pa_ref[...] = jnp.zeros_like(pa_ref)
    pb_ref[...] = jnp.zeros_like(pb_ref)
    mine, other = sent_ref[pl.ds(Z_THREE, 1)], za_ref[pl.ds(Z_THREE, 1)]
    pa_ref[pl.ds(Y_THREE, 1)] = jnp.where(
        iota((1, 512), 1) // 128 % 2 == ids_ref[2], mine, other
    )

    def get(level, x, y, z):
        n = level_extent(level)
        if z < 0:
            return zl[pl.ds(z_row(level, x, y), 1)]
        if z >= n:
            return zh[pl.ds(z_row(level, x, y), 1)]
        return own_ref[pl.ds(own_row(level, x, y, z), 1)]

    for level in (6, 5, 4):
        n = level_extent(level)
        for z in range(-1, n + 1):
            for x in range(n):
                low, high = get(level, x, 0, z), get(level, x, n - 1, z)
                i = y_row(level, x, z)
                pa_ref[pl.ds(i, 1)] = jnp.where(odd, low, high)
                pb_ref[pl.ds(i, 1)] = jnp.where(odd, high, low)


def x_kernel(ids_ref, own_ref, zb_ref, za_ref, ya_ref, yb_ref, pa_ref, pb_ref, zl, zh, yl, yh):
    sort_sides(ids_ref[2] == 1, za_ref, zb_ref, zl, zh)
    sort_sides(ids_ref[1] == 1, ya_ref, yb_ref, yl, yh)
    odd = ids_ref[0] == 1
    pa_ref[...] = jnp.zeros_like(pa_ref)
    pb_ref[...] = jnp.zeros_like(pb_ref)

    def get(level, x, y, z):
        n = level_extent(level)
        if y < 0:
            return yl[pl.ds(y_row(level, x, z), 1)]
        if y >= n:
            return yh[pl.ds(y_row(level, x, z), 1)]
        if z < 0:
            return zl[pl.ds(z_row(level, x, y), 1)]
        if z >= n:
            return zh[pl.ds(z_row(level, x, y), 1)]
        return own_ref[pl.ds(own_row(level, x, y, z), 1)]

    for level in (6, 5, 4):
        n = level_extent(level)
        for z in range(-1, n + 1):
            for y in range(-1, n + 1):
                low, high = get(level, 0, y, z), get(level, n - 1, y, z)
                i = x_row(level, y, z)
                pa_ref[pl.ds(i, 1)] = jnp.where(odd, low, high)
                pb_ref[pl.ds(i, 1)] = jnp.where(odd, high, low)


def coarse_rows(quads):
    half = iota((128, 128), 1) // 64
    keep = half == iota((128, 128), 0) % 2
    blocks = []
    for i in range(4):
        pair = quads[:, 128 * (i // 2) : 128 * (i // 2) + 128]
        both = jnp.where(half == i % 2, pair, pltpu.roll(pair, 64, 1))
        blocks.append(jnp.where(keep, both, 0.0))
    gather = jnp.where(iota((64, 128), 0) == iota((64, 128), 1) // 2, 1.0, 0.0).astype(BF16)
    return exact_times(gather, jnp.concatenate(blocks, axis=1))


def place_mix(wide, j, ky, kz, mix, row):
    rows, half = mix.shape[0], wide.shape[1] // 2
    high, low = split(mix)
    for t in range(4):
        c = source_class(t, ky, kz)
        wide[t, row : row + rows, 128 * j : 128 * j + 128] = high[:, 128 * c : 128 * c + 128]
        wide[t, half + row : half + row + rows, 128 * j : 128 * j + 128] = low[:, 128 * c : 128 * c + 128]


def far_rows(wide, far_ref, dx):
    parts = []
    for t in range(4):
        rows = 1152 * (4 * dx + t)
        product = mm(wide[t], far_ref[rows : rows + 1152])
        half = product.shape[0] // 2
        top, bottom = product[:half], product[half:]
        parts.append((top[:, :128] + bottom[:, :128]) + (top[:, 128:] + bottom[:, 128:]))
    return jnp.concatenate(parts, axis=1)


def reflected(rows):
    return jnp.where(iota(rows.shape, 1) // 64 % 2 == 1, -rows, rows)


def whole_down(down_ref):
    return jnp.concatenate([down_ref[128 * i : 128 * i + 128] for i in range(4)], axis=1)


def only(row, octant):
    kept = iota((8, 512), 1) // 64 == octant
    return jnp.where(kept, jnp.broadcast_to(row, (8, 512)), 0.0)


def inner_kernel(
    ids_ref, own_ref, zb_ref, za_ref, ya_ref, yb_ref, blob, out_ref, up_ref, basis_ref, coarse_ref, rim_ref,
    fine_src, small_src, wide_zero, wide_one, small_ref, fine_ref, far_ref, sem,
):
    later = [
        piece_copy(blob, "up", up_ref, sem.at[4]),
        piece_copy(blob, "basis", basis_ref, sem.at[5]),
        piece_copy(blob, "coarse", coarse_ref, sem.at[6], ids_ref[3], 64),
        piece_copy(blob, "rim", rim_ref, sem.at[7]),
    ]
    small_copy = piece_copy(blob, "small", small_ref, sem.at[0])
    fine_copy = piece_copy(blob, "fine", fine_ref, sem.at[1])
    tables = [piece_copy(blob, "far", far_ref, sem.at[2 + dx], dx, 2) for dx in range(2)]
    for copy in (small_copy, fine_copy, *tables, *later):
        copy.start()
    fine_src[144:] = jnp.zeros((112, 512), F32)
    small_src[64:] = jnp.zeros((64, 512), F32)
    stack = [own_ref[...]]
    for axis, ra_ref, rb_ref in ((2, za_ref, zb_ref), (1, ya_ref, yb_ref)):
        odd = ids_ref[axis] == 1
        a, b = ra_ref[...], rb_ref[...]
        stack += [jnp.where(odd, a, b), jnp.where(odd, b, a)]
    for target, parts in ((fine_src, FINE_PARTS), (small_src, SMALL_PARTS)):
        base = 0
        for values, (start, stop) in zip(stack, parts):
            target[base : base + stop - start] = values[start:stop]
            base += stop - start
    small_copy.wait()
    small = exact_times(small_ref[:, :128], small_src[...])
    fine_split = jnp.concatenate(split(fine_src[...]), axis=1)
    fine_copy.wait()
    far = 0.0
    for group in (1, 0, 2):
        mixes = mm(fine_ref[576 * group : 576 * group + 576], fine_split)
        mixes = mixes[:, :512] + mixes[:, 512:]
        for j in range(9):
            k = 9 * group + j
            _, ky, kz = KINDS[k]
            mix = [mixes[64 * j : 64 * j + 64], small[SMALL * k : SMALL * k + SMALL]]
            mix = jnp.concatenate(mix, axis=0)
            if group == 1:
                place_mix(wide_zero, j, ky, kz, mix, 0)
            else:
                mix = reflected(mix) if group == 0 else mix
                place_mix(wide_one, j, ky, kz, mix, ROWS if group == 0 else 0)
        if group == 1:
            tables[0].wait()
            far = far_rows(wide_zero, far_ref, 0)
    tables[1].wait()
    both = far_rows(wide_one, far_ref, 1)
    out_ref[...] = far + both[:ROWS] + reflected(both[ROWS:])
    for copy in later:
        copy.wait()


def outer_kernel(
    ids_ref, far_in_ref, xa_ref, xb_ref, quads_ref, mask_ref, up_ref, basis_ref, coarse_ref, rim_ref, blob, out_ref,
    wide_zero, wide_one, far_ref, spot_ref, back_ref, down_ref, sem,
):
    tables = [piece_copy(blob, "far", far_ref, sem.at[dx], dx, 2) for dx in range(2)]
    last = [
        piece_copy(blob, "spot", spot_ref, sem.at[2]),
        piece_copy(blob, "back", back_ref, sem.at[3]),
        piece_copy(blob, "down", down_ref, sem.at[4]),
    ]
    for copy in (*reversed(tables), *last):
        copy.start()
    three = coarse_rows(quads_ref[...].reshape(128, 256))
    odd = ids_ref[0] == 1
    a, b = xa_ref[...], xb_ref[...]
    low, high = jnp.where(odd, a, b), jnp.where(odd, b, a)
    sides = jnp.concatenate([*split(high), *split(reflected(low))], axis=1)
    two = up_group(three, up_ref[...])
    mixes = mm(rim_ref[:, :X_ROWS], sides)
    upper = jnp.concatenate([three, two, jnp.zeros((56, 512), F32)], axis=0)
    upper = times_exact(upper, in_columns(basis_ref))
    chosen = jnp.concatenate([coarse_ref[:, :128], coarse_ref[:208, 128:]], axis=0)
    coarse = exact_times(chosen, upper)
    for side in range(2):
        mix = mixes[:, 1024 * side : 1024 * side + 512] + mixes[:, 1024 * side + 512 : 1024 * side + 1024]
        for j in range(9):
            _, ky, kz = KINDS[j]
            place_mix(wide_one, j, ky, kz, mix[RIM * j : RIM * j + RIM], RIM * side)
    for k, (dx, ky, kz) in enumerate(KINDS):
        mix = coarse[SMALL * k : SMALL * k + SMALL]
        if dx == 0:
            place_mix(wide_zero, k % 9, ky, kz, mix, 0)
        elif dx == 1:
            place_mix(wide_one, k % 9, ky, kz, mix, 2 * RIM)
        else:
            place_mix(wide_one, k % 9, ky, kz, reflected(mix), 2 * RIM + SMALL)
    tables[1].wait()
    one = far_rows(wide_one, far_ref, 1)
    tables[0].wait()
    zero = far_rows(wide_zero, far_ref, 0)
    rims = jnp.concatenate([one[:RIM], reflected(one[RIM : 2 * RIM])], axis=0)
    small = zero + one[2 * RIM : 2 * RIM + SMALL] + reflected(one[2 * RIM + SMALL :])
    for copy in last:
        copy.wait()
    far = far_in_ref[...] + exact_times(spot_ref[:, : 2 * RIM], rims)
    far = jnp.concatenate([far[:64], far[64:] + small], axis=0)
    far = times_exact(far, in_columns(back_ref))
    down = whole_down(down_ref)
    local = far[73:74] + downward(only(far[74:75], ids_ref[4]), down)
    local = far[72:73] + downward(only(local[:1], ids_ref[5]), down)
    local = jnp.broadcast_to(local[:1], (8, 512)) * octant_mask(8)
    local = far[64:72] + downward(local, down)
    local = jnp.broadcast_to(local[:, None, :], (8, 8, 512)).reshape(64, 512) * octant_mask(64)
    out_ref[...] = (far[:64] + downward(local, down)) * mask_ref[...]


def pairs(axis, outer):
    result = []
    for i in range(512):
        c = place(i, 3)
        c[axis] = (c[axis] ^ 1) if not outer else c[axis] + (1 if c[axis] % 2 else -1)
        if 0 <= c[axis] < 8:
            result.append((i, morton(*c, 3)))
    return result


def exchange(pa, pb, axis):
    return (
        lax.ppermute(pa, AXES, pairs(axis, False)),
        lax.ppermute(pb, AXES, pairs(axis, True)),
    )


SMEM = pl.BlockSpec(memory_space=pltpu.SMEM)
VMEM = pl.BlockSpec(memory_space=pltpu.VMEM)
HBM = pl.BlockSpec(memory_space=pltpu.HBM)
AXES = ("upper", "bit2", "bit1", "bit0")
LIMIT = 52 * 2**20


def call(kernel, shapes, scratch, ids, vmem_args, hbm_args=(), micros=1):
    return pl.pallas_call(
        kernel,
        out_shape=[jax.ShapeDtypeStruct(shape[:2], (*shape, F32)[2]) for shape in shapes],
        in_specs=[SMEM] + [VMEM] * len(vmem_args) + [HBM] * len(hbm_args),
        out_specs=[VMEM] * len(shapes),
        scratch_shapes=scratch,
        compiler_params=pltpu.CompilerParams(vmem_limit_bytes=LIMIT),
        cost_estimate=pl.CostEstimate(flops=micros * 10**9, bytes_accessed=0, transcendentals=0),
    )(ids, *vmem_args, *hbm_args)


def rows_of(*counts):
    return [(count, 512) for count in counts]


def scratch_rows(*counts):
    return [pltpu.VMEM((count, 512), F32) for count in counts]


def table_scratch(*names):
    return [pltpu.VMEM((PIECES[name], 256), BF16) for name in names]


def wide_scratch(*shape):
    return [pltpu.VMEM(shape, BF16)]


def local(multipoles, occupancy):
    blob = jnp.asarray(constants())
    me = lax.axis_index(AXES)
    parent = me // 8
    ids = jnp.stack([me % 2, me // 2 % 2, me // 4 % 2, parent, parent % 8, me % 8]).astype(jnp.int32)
    own, pa, pb, mask = call(
        upward_kernel,
        rows_of(ROWS, Z_ROWS, Z_ROWS, 64),
        table_scratch("up", "basis") + [pltpu.SemaphoreType.DMA((2,))],
        ids, [multipoles, occupancy.reshape(1, 512)], [blob], micros=4,
    )
    za, zb = exchange(pa, pb, 2)
    pa, pb = call(
        y_kernel, rows_of(Y_ROWS, Y_ROWS), scratch_rows(Z_ROWS, Z_ROWS), ids, [own, pa, zb, za]
    )
    ya, yb = exchange(pa, pb, 1)
    ours, theirs = (p[Y_THREE : Y_THREE + 1, :256] for p in (pa, ya))
    quad = jnp.where(jnp.arange(256)[None] // 64 % 2 == ids[1], ours, theirs)
    quads = lax.all_to_all(
        jnp.broadcast_to(quad[None], (128, 1, 256)), ("upper", "bit0"), 0, 0, tiled=True
    )
    pa, pb = call(
        x_kernel, rows_of(X_ROWS, X_ROWS), scratch_rows(Z_ROWS, Z_ROWS, Y_ROWS, Y_ROWS),
        ids, [own, zb, za, ya, yb], micros=40,
    )
    xa, xb = exchange(pa, pb, 0)
    far, *tables = call(
        inner_kernel,
        rows_of(ROWS) + [(PIECES[n] // (64 if n == "coarse" else 1), 256, BF16) for n in TABLES],
        scratch_rows(256, 128)
        + wide_scratch(4, 2 * ROWS, 9 * 128)
        + wide_scratch(4, 4 * ROWS, 9 * 128)
        + table_scratch("small", "fine", "far")
        + [pltpu.SemaphoreType.DMA((8,))],
        ids, [own, zb, za, ya, yb], [blob], micros=1,
    )
    (out,) = call(
        outer_kernel,
        rows_of(64),
        wide_scratch(4, 2 * SMALL, 9 * 128)
        + wide_scratch(4, 4 * RIM + 4 * SMALL, 9 * 128)
        + table_scratch("far", "spot", "back", "down")
        + [pltpu.SemaphoreType.DMA((5,))],
        ids, [far, xa, xb, quads, mask, *tables], [blob], micros=4,
    )
    return out


def solution(mesh):
    fine_mesh = Mesh(mesh.devices.reshape(64, 2, 2, 2), AXES)
    return jax.shard_map(
        local,
        mesh=fine_mesh,
        in_specs=(P(AXES, None), P(AXES)),
        out_specs=P(AXES, None),
        check_vma=False,
    )
```

```python
import functools

import jax
import jax.numpy as jnp
import ml_dtypes
import numpy as np
from jax import lax
from jax.experimental import pallas as pl
from jax.experimental.pallas import tpu as pltpu
from jax.sharding import Mesh
from jax.sharding import PartitionSpec as P

F32 = jnp.float32
BF16 = jnp.bfloat16
NODES = np.cos((2.0 * np.arange(4) + 1.0) * (np.pi / 8.0))
ENTRY = np.arange(512)
OCT = [ENTRY // 64 % 2, ENTRY // 128 % 2, ENTRY // 256 % 2]
DEG = [ENTRY // 16 % 4, ENTRY // 4 % 4, ENTRY % 4]
KINDS = [(dx, ky, kz) for dx in (-1, 0, 1) for ky in range(3) for kz in range(3)]
ROWS = 80
SMALL = 16
PIECES = {
    "up": 512, "basis": 1024, "small": 432, "fine": 1728, "rim": 288, "spot": 80, "far": 9216,
    "back": 1024, "down": 512, "coarse": 64 * 224,
}
TABLES = ("up", "basis", "coarse", "rim")


def halves(values):
    high = values.astype(np.float32).astype(ml_dtypes.bfloat16)
    low = (values - high.astype(np.float64)).astype(ml_dtypes.bfloat16)
    return high, low


def table(shift):
    distance = np.zeros((512, 512))
    reach = np.zeros((512, 512), int)
    for d in range(3):
        offset = 2 * shift[d] + OCT[d][:, None] - OCT[d][None, :]
        reach = np.maximum(reach, abs(offset))
        placed = NODES[DEG[d]]
        distance += (offset + 0.5 * (placed[:, None] - placed[None, :])) ** 2
    keep = reach >= 2
    return np.where(keep, 1.0 / np.sqrt(np.where(keep, distance, 1.0)), 0.0)


def upward_matrix():
    def terms(v):
        return [v, 2 * v * v - 1, 4 * v**3 - 3 * v]

    parent = np.arange(64)
    degrees = [parent // 16, parent // 4 % 4, parent % 4]
    result = np.ones((512, 64))
    for d in range(3):
        child = (OCT[d] - 0.5 + 0.5 * NODES[DEG[d]])[:, None]
        place = NODES[degrees[d]][None, :]
        result *= 0.25 + 0.5 * sum(a * b for a, b in zip(terms(place), terms(child)))
    return result


def parity_signs():
    signs = np.zeros((512, 512))
    for q in range(512):
        odd = [q // 64 % 2, q // 128 % 2, q // 256]
        degree = [q // 16 % 4, q // 4 % 4, q % 4]
        for o in range(8):
            octant = [o % 2, o // 2 % 2, o // 4]
            a, b, e = (3 - v if side else v for v, side in zip(degree, octant))
            sign = (-1) ** sum(c * side for c, side in zip(odd, octant))
            signs[64 * o + 16 * a + 4 * b + e, q] = sign
    return signs


def morton(x, y, z, bits):
    return sum(
        (x >> i & 1) << 3 * i | (y >> i & 1) << 3 * i + 1 | (z >> i & 1) << 3 * i + 2
        for i in range(bits)
    )


def place(number, bits):
    return [sum((number >> 3 * i + d & 1) << i for i in range(bits)) for d in range(3)]


Z_ROWS, Y_ROWS, X_ROWS = 24, 40, 64
Z_THREE, Y_THREE = 21, 35
FINE_PARTS = ((0, 64), (0, 16), (0, 16), (0, 24), (0, 24))
SMALL_PARTS = ((64, 80), (16, 24), (16, 24), (24, 40), (24, 40))
RIM = 32


def level_extent(level):
    return 2 ** (level - 4)


def own_row(level, x, y, z):
    return {6: 0, 5: 64, 4: 72}[level] + morton(x, y, z, level - 4)


def z_row(level, x, y):
    n = level_extent(level)
    return {6: 0, 5: 16, 4: 20}[level] + y * n + x


def y_row(level, x, z):
    n = level_extent(level)
    return {6: 0, 5: 24, 4: 32}[level] + (z + 1) * n + x


def x_row(level, y, z):
    n = level_extent(level) + 2
    return {6: 0, 5: 36, 4: 52}[level] + (z + 1) * n + y + 1


def source_row(level, x, y, z):
    n = level_extent(level)
    if not 0 <= y < n:
        part, row = (4 if y >= n else 3), y_row(level, x, z)
    elif not 0 <= z < n:
        part, row = (2 if z >= n else 1), z_row(level, x, y)
    else:
        part, row = 0, own_row(level, x, y, z)
    parts = FINE_PARTS if level == 6 else SMALL_PARTS
    start, stop = parts[part]
    assert start <= row < stop
    return sum(q - p for p, q in parts[:part]) + row - start


def kind_terms(kind):
    return [(0, 1)] if kind == 0 else [(1, 1), (-1, 1 if kind == 1 else -1)]


def rim_target(level, y, z):
    return {6: 0, 5: 16, 4: 20}[level] + z * level_extent(level) + y


def selections():
    fine = np.zeros((27, 64, 256))
    small = np.zeros((27, SMALL, 128))
    rim = np.zeros((9, RIM, 256))
    spot = np.zeros((ROWS, 256))
    for k, (dx, ky, kz) in enumerate(KINDS):
        for dy, sy in kind_terms(ky):
            for dz, sz in kind_terms(kz):
                for level in (6, 5, 4):
                    n = level_extent(level)
                    factor = sy * sz * 2.0 ** (level - 6)
                    into = fine[k] if level == 6 else small[k]
                    for m in range(n**3):
                        x, y, z = place(m, level - 4)
                        row = own_row(level, x, y, z) % 64
                        if 0 <= x + dx < n:
                            into[row, source_row(level, x + dx, y + dy, z + dz)] += factor
                        elif dx == 1:
                            rim[k - 18, rim_target(level, y, z), x_row(level, y + dy, z + dz)] += factor
                            spot[own_row(level, x, y, z), rim_target(level, y, z)] = 1
                        else:
                            spot[own_row(level, x, y, z), RIM + rim_target(level, y, z)] = 1
    coarse = np.zeros((64, 27, SMALL, 128))
    for parent in range(64):
        for level, row, base in ((3, 9, 0), (2, 10, 64)):
            bits = level - 1
            n = 2**bits
            x, y, z = place(parent >> 3 * (2 - bits), bits)
            for k, (dx, ky, kz) in enumerate(KINDS):
                for dy, sy in kind_terms(ky):
                    for dz, sz in kind_terms(kz):
                        u = (x + dx, y + dy, z + dz)
                        if all(0 <= c < n for c in u):
                            coarse[parent, k, row, base + morton(*u, bits)] += (
                                sy * sz * 2.0 ** (level - 6)
                            )
    coarse = np.pad(coarse.reshape(64, 27 * SMALL, 128), ((0, 0), (0, 16), (0, 0)))
    return {
        "small": np.pad(small.reshape(27 * SMALL, 128), ((0, 0), (0, 128))),
        "fine": fine.reshape(27 * 64, 256),
        "rim": rim.reshape(9 * RIM, 256),
        "spot": spot,
        "coarse": np.concatenate(np.split(coarse, 2, axis=1), axis=2).reshape(64 * 224, 256),
    }


@functools.lru_cache(maxsize=1)
def constants():
    basis, back = 0.5 * parity_signs(), 0.25 * parity_signs().T
    tables = {
        (dx, dy, dz): back @ table((dx, dy, dz)) @ basis
        for dx in (0, 1)
        for dy in (0, 1)
        for dz in (0, 1)
    }
    far = np.zeros((2, 4, 9 * 128, 256), ml_dtypes.bfloat16)
    for t in range(4):
        for k, (dx, ky, kz) in enumerate(KINDS[9:]):
            c = source_class(t, ky, kz)
            block = tables[dx, min(ky, 1), min(kz, 1)][
                128 * c : 128 * c + 128, 128 * t : 128 * t + 128
            ]
            high, low = halves(block)
            j = 128 * (k % 9)
            far[dx, t, j : j + 128, :128] = high
            far[dx, t, j : j + 128, 128:] = low
    up = upward_matrix()
    wide_down = np.concatenate(halves(np.tile(up.T, (2, 1))), axis=1)
    pieces = selections() | {
        "up": np.concatenate(halves(np.tile(up, (1, 2))), axis=1),
        "basis": in_lanes(basis),
        "far": far.reshape(-1, 256),
        "back": in_lanes(back),
        "down": in_lanes(wide_down),
    }
    assert {name: len(piece) for name, piece in pieces.items()} == PIECES
    return np.concatenate([pieces[name].astype(ml_dtypes.bfloat16) for name in PIECES])


def in_lanes(matrix):
    return np.concatenate(np.split(matrix, matrix.shape[1] // 256, axis=1))


def source_class(t, ky, kz):
    return t ^ ((ky == 2) | (kz == 2) << 1)


def split(values):
    high = values.astype(BF16)
    return high, (values - high.astype(F32)).astype(BF16)


def mm(a, b):
    return jnp.dot(a, b, preferred_element_type=F32)


def stacked(values):
    rows, width = values.shape
    if rows % 16:
        values = jnp.concatenate([values, jnp.zeros((16 - rows % 16, width), F32)], axis=0)
    return jnp.concatenate(split(values), axis=0)


def times_exact(values, matrix):
    product = mm(stacked(values), matrix)
    half = product.shape[0] // 2
    return (product[:half] + product[half:])[: values.shape[0]]


def times_pair(values, matrix):
    product = mm(stacked(values), matrix)
    half = product.shape[0] // 2
    width = product.shape[1] // 2
    total = product[:half, :width] + product[half:, :width] + product[:half, width:]
    return total[: values.shape[0]]


def exact_times(matrix, values):
    product = mm(matrix, jnp.concatenate(split(values), axis=1))
    width = values.shape[1]
    return product[:, :width] + product[:, width:]


def piece_copy(blob, name, ref, sem, part=0, parts=1):
    start = sum(list(PIECES.values())[: list(PIECES).index(name)])
    rows = PIECES[name] // parts
    source = blob.at[pl.ds(pl.multiple_of(start + part * rows, 16), rows)]
    target = ref if ref.shape[0] == rows else ref.at[pl.ds(part * rows, rows)]
    return pltpu.make_async_copy(source, target, sem)


def in_columns(ref):
    rows = ref.shape[0] // 2
    return jnp.concatenate([ref[:rows], ref[rows:]], axis=1)


def iota(shape, axis):
    return lax.broadcasted_iota(jnp.int32, shape, axis)


def octant_mask(rows):
    return (iota((rows, 512), 1) // 64 == iota((rows, 512), 0) % 8).astype(F32)


def occupancy_mask(occ):
    kept = jnp.where(
        iota((64, 512), 1) // 8 == iota((64, 512), 0), jnp.broadcast_to(occ.astype(F32), (64, 512)), 0.0
    )
    spread = iota((512, 512), 0) % 8 == iota((512, 512), 1) // 64
    return mm(kept.astype(BF16), jnp.where(spread, 1.0, 0.0).astype(BF16))


def upward(values, up):
    twice = times_pair(values, up)
    return jnp.concatenate([twice] * 4, axis=1)


def up_group(values, up):
    rows = values.shape[0]
    return (upward(values, up) * octant_mask(rows)).reshape(rows // 8, 8, 512).sum(axis=1)


def downward(masked, down):
    folded = masked[:, :128] + masked[:, 128:256] + masked[:, 256:384] + masked[:, 384:]
    return times_pair(folded, down)


def upward_kernel(
    ids_ref, mult_ref, occ_ref, blob, own_ref, pa_ref, pb_ref, mask_ref, up_ref, basis_ref, sem
):
    up_copy = piece_copy(blob, "up", up_ref, sem.at[0])
    basis_copy = piece_copy(blob, "basis", basis_ref, sem.at[1])
    up_copy.start()
    basis_copy.start()
    mask_ref[...] = occupancy_mask(occ_ref[...])
    up_copy.wait()
    grouped_six = mult_ref[...] * mask_ref[...]
    grouped_five = up_group(grouped_six, up_ref[...])
    grouped_four = up_group(grouped_five, up_ref[...])
    three = upward(jnp.broadcast_to(grouped_four, (8, 512)), up_ref[...])
    basis_copy.wait()
    basis = in_columns(basis_ref)
    own_ref[0:64] = times_exact(grouped_six, basis)
    rest = jnp.concatenate([grouped_five, jnp.broadcast_to(grouped_four, (8, 512))], axis=0)
    own_ref[64:80] = times_exact(rest, basis)
    odd = ids_ref[2] == 1
    for p_ref in (pa_ref, pb_ref):
        p_ref[Z_ROWS - 8 :] = three
    for level in (6, 5, 4):
        n = level_extent(level)
        for y in range(n):
            for x in range(n):
                low = own_ref[pl.ds(own_row(level, x, y, 0), 1)]
                high = own_ref[pl.ds(own_row(level, x, y, n - 1), 1)]
                i = z_row(level, x, y)
                pa_ref[pl.ds(i, 1)] = jnp.where(odd, low, high)
                pb_ref[pl.ds(i, 1)] = jnp.where(odd, high, low)


def sort_sides(odd, ra_ref, rb_ref, low_ref, high_ref):
    a, b = ra_ref[...], rb_ref[...]
    low_ref[...] = jnp.where(odd, a, b)
    high_ref[...] = jnp.where(odd, b, a)


def y_kernel(ids_ref, own_ref, sent_ref, zb_ref, za_ref, pa_ref, pb_ref, zl, zh):
    sort_sides(ids_ref[2] == 1, za_ref, zb_ref, zl, zh)
    odd = ids_ref[1] == 1
    pa_ref[...] = jnp.zeros_like(pa_ref)
    pb_ref[...] = jnp.zeros_like(pb_ref)
    mine, other = sent_ref[pl.ds(Z_THREE, 1)], za_ref[pl.ds(Z_THREE, 1)]
    pa_ref[pl.ds(Y_THREE, 1)] = jnp.where(
        iota((1, 512), 1) // 128 % 2 == ids_ref[2], mine, other
    )

    def get(level, x, y, z):
        n = level_extent(level)
        if z < 0:
            return zl[pl.ds(z_row(level, x, y), 1)]
        if z >= n:
            return zh[pl.ds(z_row(level, x, y), 1)]
        return own_ref[pl.ds(own_row(level, x, y, z), 1)]

    for level in (6, 5, 4):
        n = level_extent(level)
        for z in range(-1, n + 1):
            for x in range(n):
                low, high = get(level, x, 0, z), get(level, x, n - 1, z)
                i = y_row(level, x, z)
                pa_ref[pl.ds(i, 1)] = jnp.where(odd, low, high)
                pb_ref[pl.ds(i, 1)] = jnp.where(odd, high, low)


def x_kernel(ids_ref, own_ref, zb_ref, za_ref, ya_ref, yb_ref, pa_ref, pb_ref, zl, zh, yl, yh):
    sort_sides(ids_ref[2] == 1, za_ref, zb_ref, zl, zh)
    sort_sides(ids_ref[1] == 1, ya_ref, yb_ref, yl, yh)
    odd = ids_ref[0] == 1
    pa_ref[...] = jnp.zeros_like(pa_ref)
    pb_ref[...] = jnp.zeros_like(pb_ref)

    def get(level, x, y, z):
        n = level_extent(level)
        if y < 0:
            return yl[pl.ds(y_row(level, x, z), 1)]
        if y >= n:
            return yh[pl.ds(y_row(level, x, z), 1)]
        if z < 0:
            return zl[pl.ds(z_row(level, x, y), 1)]
        if z >= n:
            return zh[pl.ds(z_row(level, x, y), 1)]
        return own_ref[pl.ds(own_row(level, x, y, z), 1)]

    for level in (6, 5, 4):
        n = level_extent(level)
        for z in range(-1, n + 1):
            for y in range(-1, n + 1):
                low, high = get(level, 0, y, z), get(level, n - 1, y, z)
                i = x_row(level, y, z)
                pa_ref[pl.ds(i, 1)] = jnp.where(odd, low, high)
                pb_ref[pl.ds(i, 1)] = jnp.where(odd, high, low)


def coarse_rows(quads):
    half = iota((128, 128), 1) // 64
    keep = half == iota((128, 128), 0) % 2
    blocks = []
    for i in range(4):
        pair = quads[:, 128 * (i // 2) : 128 * (i // 2) + 128]
        both = jnp.where(half == i % 2, pair, pltpu.roll(pair, 64, 1))
        blocks.append(jnp.where(keep, both, 0.0))
    gather = jnp.where(iota((64, 128), 0) == iota((64, 128), 1) // 2, 1.0, 0.0).astype(BF16)
    return exact_times(gather, jnp.concatenate(blocks, axis=1))


def place_mix(wide, j, ky, kz, mix, row):
    rows, half = mix.shape[0], wide.shape[1] // 2
    high, low = split(mix)
    for t in range(4):
        c = source_class(t, ky, kz)
        wide[t, row : row + rows, 128 * j : 128 * j + 128] = high[:, 128 * c : 128 * c + 128]
        wide[t, half + row : half + row + rows, 128 * j : 128 * j + 128] = low[:, 128 * c : 128 * c + 128]


def far_rows(wide, far_ref, dx):
    parts = []
    for t in range(4):
        rows = 1152 * (4 * dx + t)
        product = mm(wide[t], far_ref[rows : rows + 1152])
        half = product.shape[0] // 2
        top, bottom = product[:half], product[half:]
        parts.append((top[:, :128] + bottom[:, :128]) + (top[:, 128:] + bottom[:, 128:]))
    return jnp.concatenate(parts, axis=1)


def reflected(rows):
    return jnp.where(iota(rows.shape, 1) // 64 % 2 == 1, -rows, rows)


def whole_down(down_ref):
    return jnp.concatenate([down_ref[128 * i : 128 * i + 128] for i in range(4)], axis=1)


def only(row, octant):
    kept = iota((8, 512), 1) // 64 == octant
    return jnp.where(kept, jnp.broadcast_to(row, (8, 512)), 0.0)


def inner_kernel(
    ids_ref, own_ref, zb_ref, za_ref, ya_ref, yb_ref, blob, out_ref, up_ref, basis_ref, coarse_ref, rim_ref,
    fine_src, small_src, wide_zero, wide_one, small_ref, fine_ref, far_ref, sem,
):
    later = [
        piece_copy(blob, "up", up_ref, sem.at[4]),
        piece_copy(blob, "basis", basis_ref, sem.at[5]),
        piece_copy(blob, "coarse", coarse_ref, sem.at[6], ids_ref[3], 64),
        piece_copy(blob, "rim", rim_ref, sem.at[7]),
    ]
    small_copy = piece_copy(blob, "small", small_ref, sem.at[0])
    fine_copy = piece_copy(blob, "fine", fine_ref, sem.at[1])
    tables = [piece_copy(blob, "far", far_ref, sem.at[2 + dx], dx, 2) for dx in range(2)]
    for copy in (small_copy, fine_copy, *tables, *later):
        copy.start()
    fine_src[144:] = jnp.zeros((112, 512), F32)
    small_src[64:] = jnp.zeros((64, 512), F32)
    stack = [own_ref[...]]
    for axis, ra_ref, rb_ref in ((2, za_ref, zb_ref), (1, ya_ref, yb_ref)):
        odd = ids_ref[axis] == 1
        a, b = ra_ref[...], rb_ref[...]
        stack += [jnp.where(odd, a, b), jnp.where(odd, b, a)]
    for target, parts in ((fine_src, FINE_PARTS), (small_src, SMALL_PARTS)):
        base = 0
        for values, (start, stop) in zip(stack, parts):
            target[base : base + stop - start] = values[start:stop]
            base += stop - start
    small_copy.wait()
    small = exact_times(small_ref[:, :128], small_src[...])
    fine_split = jnp.concatenate(split(fine_src[...]), axis=1)
    fine_copy.wait()
    far = 0.0
    for group in (1, 0, 2):
        mixes = mm(fine_ref[576 * group : 576 * group + 576], fine_split)
        mixes = mixes[:, :512] + mixes[:, 512:]
        for j in range(9):
            k = 9 * group + j
            _, ky, kz = KINDS[k]
            mix = [mixes[64 * j : 64 * j + 64], small[SMALL * k : SMALL * k + SMALL]]
            mix = jnp.concatenate(mix, axis=0)
            if group == 1:
                place_mix(wide_zero, j, ky, kz, mix, 0)
            else:
                mix = reflected(mix) if group == 0 else mix
                place_mix(wide_one, j, ky, kz, mix, ROWS if group == 0 else 0)
        if group == 1:
            tables[0].wait()
            far = far_rows(wide_zero, far_ref, 0)
    tables[1].wait()
    both = far_rows(wide_one, far_ref, 1)
    out_ref[...] = far + both[:ROWS] + reflected(both[ROWS:])
    for copy in later:
        copy.wait()


def outer_kernel(
    ids_ref, far_in_ref, xa_ref, xb_ref, quads_ref, mask_ref, up_ref, basis_ref, coarse_ref, rim_ref, blob, out_ref,
    wide_zero, wide_one, far_ref, spot_ref, back_ref, down_ref, sem,
):
    tables = [piece_copy(blob, "far", far_ref, sem.at[dx], dx, 2) for dx in range(2)]
    last = [
        piece_copy(blob, "spot", spot_ref, sem.at[2]),
        piece_copy(blob, "back", back_ref, sem.at[3]),
        piece_copy(blob, "down", down_ref, sem.at[4]),
    ]
    for copy in (*reversed(tables), *last):
        copy.start()
    three = coarse_rows(quads_ref[...].reshape(128, 256))
    odd = ids_ref[0] == 1
    a, b = xa_ref[...], xb_ref[...]
    low, high = jnp.where(odd, a, b), jnp.where(odd, b, a)
    sides = jnp.concatenate([*split(high), *split(reflected(low))], axis=1)
    two = up_group(three, up_ref[...])
    mixes = mm(rim_ref[:, :X_ROWS], sides)
    upper = jnp.concatenate([three, two, jnp.zeros((56, 512), F32)], axis=0)
    upper = times_exact(upper, in_columns(basis_ref))
    chosen = jnp.concatenate([coarse_ref[:, :128], coarse_ref[:208, 128:]], axis=0)
    coarse = exact_times(chosen, upper)
    for side in range(2):
        mix = mixes[:, 1024 * side : 1024 * side + 512] + mixes[:, 1024 * side + 512 : 1024 * side + 1024]
        for j in range(9):
            _, ky, kz = KINDS[j]
            place_mix(wide_one, j, ky, kz, mix[RIM * j : RIM * j + RIM], RIM * side)
    for k, (dx, ky, kz) in enumerate(KINDS):
        mix = coarse[SMALL * k : SMALL * k + SMALL]
        if dx == 0:
            place_mix(wide_zero, k % 9, ky, kz, mix, 0)
        elif dx == 1:
            place_mix(wide_one, k % 9, ky, kz, mix, 2 * RIM)
        else:
            place_mix(wide_one, k % 9, ky, kz, reflected(mix), 2 * RIM + SMALL)
    tables[1].wait()
    one = far_rows(wide_one, far_ref, 1)
    tables[0].wait()
    zero = far_rows(wide_zero, far_ref, 0)
    rims = jnp.concatenate([one[:RIM], reflected(one[RIM : 2 * RIM])], axis=0)
    small = zero + one[2 * RIM : 2 * RIM + SMALL] + reflected(one[2 * RIM + SMALL :])
    for copy in last:
        copy.wait()
    far = far_in_ref[...] + exact_times(spot_ref[:, : 2 * RIM], rims)
    far = jnp.concatenate([far[:64], far[64:] + small], axis=0)
    far = times_exact(far, in_columns(back_ref))
    down = whole_down(down_ref)
    local = far[73:74] + downward(only(far[74:75], ids_ref[4]), down)
    local = far[72:73] + downward(only(local[:1], ids_ref[5]), down)
    local = jnp.broadcast_to(local[:1], (8, 512)) * octant_mask(8)
    local = far[64:72] + downward(local, down)
    local = jnp.broadcast_to(local[:, None, :], (8, 8, 512)).reshape(64, 512) * octant_mask(64)
    out_ref[...] = (far[:64] + downward(local, down)) * mask_ref[...]


def pairs(axis, outer):
    result = []
    for i in range(512):
        c = place(i, 3)
        c[axis] = (c[axis] ^ 1) if not outer else c[axis] + (1 if c[axis] % 2 else -1)
        if 0 <= c[axis] < 8:
            result.append((i, morton(*c, 3)))
    return result


def exchange(pa, pb, axis):
    return (
        lax.ppermute(pa, AXES, pairs(axis, False)),
        lax.ppermute(pb, AXES, pairs(axis, True)),
    )


SMEM = pl.BlockSpec(memory_space=pltpu.SMEM)
VMEM = pl.BlockSpec(memory_space=pltpu.VMEM)
HBM = pl.BlockSpec(memory_space=pltpu.HBM)
AXES = ("upper", "bit2", "bit1", "bit0")
LIMIT = 52 * 2**20


def call(kernel, shapes, scratch, ids, vmem_args, hbm_args=(), micros=1):
    return pl.pallas_call(
        kernel,
        out_shape=[jax.ShapeDtypeStruct(shape[:2], (*shape, F32)[2]) for shape in shapes],
        in_specs=[SMEM] + [VMEM] * len(vmem_args) + [HBM] * len(hbm_args),
        out_specs=[VMEM] * len(shapes),
        scratch_shapes=scratch,
        compiler_params=pltpu.CompilerParams(vmem_limit_bytes=LIMIT),
        cost_estimate=pl.CostEstimate(flops=micros * 10**9, bytes_accessed=0, transcendentals=0),
    )(ids, *vmem_args, *hbm_args)


def rows_of(*counts):
    return [(count, 512) for count in counts]


def scratch_rows(*counts):
    return [pltpu.VMEM((count, 512), F32) for count in counts]


def table_scratch(*names):
    return [pltpu.VMEM((PIECES[name], 256), BF16) for name in names]


def wide_scratch(*shape):
    return [pltpu.VMEM(shape, BF16)]


def local(multipoles, occupancy):
    blob = jnp.asarray(constants())
    me = lax.axis_index(AXES)
    parent = me // 8
    ids = jnp.stack([me % 2, me // 2 % 2, me // 4 % 2, parent, parent % 8, me % 8]).astype(jnp.int32)
    own, pa, pb, mask = call(
        upward_kernel,
        rows_of(ROWS, Z_ROWS, Z_ROWS, 64),
        table_scratch("up", "basis") + [pltpu.SemaphoreType.DMA((2,))],
        ids, [multipoles, occupancy.reshape(1, 512)], [blob], micros=4,
    )
    za, zb = exchange(pa, pb, 2)
    pa, pb = call(
        y_kernel, rows_of(Y_ROWS, Y_ROWS), scratch_rows(Z_ROWS, Z_ROWS), ids, [own, pa, zb, za]
    )
    ya, yb = exchange(pa, pb, 1)
    ours, theirs = (p[Y_THREE : Y_THREE + 1, :256] for p in (pa, ya))
    spread = (128, 1, 256)
    own_side = lax.broadcasted_iota(jnp.int32, spread, 2) // 64 % 2 == ids[1]
    quad = jnp.where(own_side, jnp.broadcast_to(ours[None], spread), jnp.broadcast_to(theirs[None], spread))
    quads = lax.all_to_all(quad, ("upper", "bit0"), 0, 0, tiled=True)
    pa, pb = call(
        x_kernel, rows_of(X_ROWS, X_ROWS), scratch_rows(Z_ROWS, Z_ROWS, Y_ROWS, Y_ROWS),
        ids, [own, zb, za, ya, yb], micros=40,
    )
    xa, xb = exchange(pa, pb, 0)
    far, *tables = call(
        inner_kernel,
        rows_of(ROWS) + [(PIECES[n] // (64 if n == "coarse" else 1), 256, BF16) for n in TABLES],
        scratch_rows(256, 128)
        + wide_scratch(4, 2 * ROWS, 9 * 128)
        + wide_scratch(4, 4 * ROWS, 9 * 128)
        + table_scratch("small", "fine", "far")
        + [pltpu.SemaphoreType.DMA((8,))],
        ids, [own, zb, za, ya, yb], [blob], micros=1,
    )
    (out,) = call(
        outer_kernel,
        rows_of(64),
        wide_scratch(4, 2 * SMALL, 9 * 128)
        + wide_scratch(4, 4 * RIM + 4 * SMALL, 9 * 128)
        + table_scratch("far", "spot", "back", "down")
        + [pltpu.SemaphoreType.DMA((5,))],
        ids, [far, xa, xb, quads, mask, *tables], [blob], micros=4,
    )
    return out


def solution(mesh):
    fine_mesh = Mesh(mesh.devices.reshape(64, 2, 2, 2), AXES)
    return jax.shard_map(
        local,
        mesh=fine_mesh,
        in_specs=(P(AXES, None), P(AXES)),
        out_specs=P(AXES, None),
        check_vma=False,
    )
```
